32 devices in a mesh: cell: 4 (over y, x), gene: 8 (over z, core).
Axes of the slice: x: 2, y: 2, z: 4, core: 2. Of those that a mesh axis runs over, the one named last changes fastest.
Arguments:
- counts: float32 [1024, 16384], P('cell', 'gene'), as said below
- gene_mean: float32 [16384], P('gene'), may hold values from -5 to 10
- gene_std: float32 [16384], P('gene'), may hold values from 0 to 10
Outputs:
- gram: float32 [16384, 16384], P('gene', 'cell')
The draws below stay inside these ranges and needn't reach their ends.
Inputs may be any that keep to these rules, and one draw needn't show every extreme that they name: `counts`: whole numbers; every cell has at least one count.
All inputs are finite; a program needn't handle non-finite values.
Results may differ from the reference program's by a relative error of at most 0.013.
Values may be sent and summed in bfloat16 or wider, within the bound.
No kernel may reach another device: no remote copies, remote signals or barrier semaphores. Data moves between devices by JAX's collectives and lax.ppermute only.
A program may use at most 192 MiB of HBM per device.

```python
import math
import jax
import jax.numpy as jnp
from jax import lax

GENES = 16384
CELLS = 1024
N_CELL = 4


def raw_counts(key, spread):
    key = jax.random.fold_in(key, 11)
    key_cell, key_gene, key_count, key_pick = jax.random.split(key, 4)
    cell_factor = jnp.exp(jax.random.uniform(key_cell, (CELLS, 1), jnp.float32, -math.log(spread), math.log(spread)))
    ramp = 1.0 + 2.0 * jnp.arange(GENES, dtype=jnp.float32) / GENES
    gene_factor = jnp.exp(jax.random.uniform(key_gene, (1, GENES), jnp.float32, math.log(0.05), math.log(5.0))) * ramp[None, :]
    rate = 0.5 * cell_factor * gene_factor
    counts = jax.random.poisson(key_count, rate).astype(jnp.float32)
    pick = jax.random.randint(key_pick, (CELLS,), 0, GENES)
    extra = (pick[:, None] == jnp.arange(GENES)[None, :]).astype(jnp.float32)
    return counts + extra


def log_stats(key, spread):
    counts = raw_counts(key, spread)
    library = jnp.sum(counts, axis=1, keepdims=True)
    normal = jnp.log1p(counts / library * 10000.0)
    centre = jnp.mean(normal, axis=0)
    deviation = jnp.sqrt(jnp.mean((normal - centre[None, :]) ** 2, axis=0))
    return (centre, deviation)


def draw_counts(key, part):
    spread = 3.0
    counts = raw_counts(key, spread)
    return counts


def draw_gene_mean(key, part):
    spread = 3.0
    centre, deviation = log_stats(key, spread)
    key = jax.random.fold_in(key, 23)
    shift = jax.random.uniform(key, (GENES,), jnp.float32, -0.5, 0.5)
    return (centre + shift * deviation).astype(jnp.float32)


def draw_gene_std(key, part):
    spread = 3.0
    centre, deviation = log_stats(key, spread)
    key = jax.random.fold_in(key, 29)
    factor = jnp.exp(jax.random.uniform(key, (GENES,), jnp.float32, math.log(0.8), math.log(1.25)))
    return (deviation * factor).astype(jnp.float32)


def setup_inputs(seed: int = 0) -> dict:
    keys = jax.random.split(jax.random.key(seed), 4)
    return {
        "counts": draw_counts(jax.random.fold_in(keys[3], 71), 0),
        "gene_mean": draw_gene_mean(jax.random.fold_in(keys[3], 71), 0),
        "gene_std": draw_gene_std(jax.random.fold_in(keys[3], 71), 0),
    }


def standardize(counts, gene_mean, gene_std):
    library = jnp.sum(counts, axis=1, keepdims=True)
    normal = jnp.log1p((counts / library) * 10000.0)
    spread = jnp.maximum(gene_std, 0.1)
    scaled = jnp.minimum((normal - gene_mean[None, :]) / spread[None, :], 10.0)
    return scaled.astype(jnp.bfloat16)


def reference(counts, gene_mean, gene_std):
    scaled = standardize(counts, gene_mean, gene_std)
    blocks = scaled.reshape(N_CELL, CELLS // N_CELL, GENES)

    def add_block(total, block):
        values = block.astype(jnp.float32)
        product = jnp.dot(values.T, values, precision=lax.Precision.HIGHEST)
        rounded = lax.optimization_barrier(product.astype(jnp.bfloat16))
        return total + rounded.astype(jnp.float32), None

    total, _ = lax.scan(add_block, jnp.zeros((GENES, GENES), jnp.float32), blocks)
    return total / CELLS
```

```python
import functools

import jax
import jax.numpy as jnp
import numpy as np
from jax import lax
from jax.experimental import pallas as pl
from jax.experimental.pallas import tpu as pltpu
from jax.sharding import PartitionSpec as P

CHUNKS = 4
HALVES = 2
STRIP = 128
VMEM = pl.BlockSpec(memory_space=pltpu.VMEM)


def send(x, axis, pairs):
    return lax.ppermute(x, axis, pairs)


def count_kernel(counts_ref, out_ref):
    cells, genes = counts_ref.shape
    total = counts_ref[:, :STRIP]
    for at in range(STRIP, genes, STRIP):
        total += counts_ref[:, at : at + STRIP]
    summed = jnp.sum(total, axis=1, keepdims=True)
    flat = jnp.broadcast_to(summed, (cells, STRIP)).T
    out_ref[...] = flat[:8, :]


def count_part(counts):
    cells, genes = counts.shape
    return pl.pallas_call(
        count_kernel,
        in_specs=[VMEM],
        out_specs=VMEM,
        out_shape=jax.ShapeDtypeStruct((8, cells), jnp.float32),
        cost_estimate=pl.CostEstimate(
            flops=cells * genes, bytes_accessed=4 * cells * genes, transcendentals=0
        ),
        name="count_part",
    )(counts)


def library_terms(part, outer, inner):
    total = part
    for s in range(1, inner):
        total = total + send(
            part,
            "gene",
            [
                (o * inner + i, o * inner + (i + s) % inner)
                for o in range(outer)
                for i in range(inner)
            ],
        )
    terms = [total]
    for s in range(1, outer):
        terms.append(
            send(
                total,
                "gene",
                [
                    (o * inner + i, (o + s) % outer * inner + i)
                    for o in range(outer)
                    for i in range(inner)
                ],
            )
        )
    return terms


def standardize_kernel(terms, counts_ref, mean_ref, std_ref, *refs):
    cells, genes = counts_ref.shape
    sums, blocks, rows = (
        refs[:terms],
        refs[terms : terms + CHUNKS],
        refs[terms + CHUNKS :],
    )
    library = sums[0][:1, :]
    for ref in sums[1:]:
        library = library + ref[:1, :]
    factor = jnp.broadcast_to(10000.0 / library, (STRIP, cells)).T
    width, height = genes // CHUNKS, genes // HALVES
    for q in range(CHUNKS):
        half = q * width // height
        start = q * width - half * height

        @pl.loop(0, width // STRIP)
        def _(k):
            there = pl.multiple_of(k * STRIP, STRIP)
            at = pl.ds(q * width + there, STRIP)
            normal = jnp.log1p(counts_ref[:, at] * factor)
            spread = 1.0 / jnp.maximum(std_ref[:, at], 0.1)
            scaled = jnp.minimum((normal - mean_ref[:, at]) * spread, 10.0)
            blocks[q][:, pl.ds(there, STRIP)] = scaled.astype(jnp.bfloat16)
            rows[half][pl.ds(start + there, STRIP), :] = scaled.T.astype(jnp.bfloat16)


def standardize(counts, terms, gene_mean, gene_std):
    cells, genes = counts.shape
    block = jax.ShapeDtypeStruct((cells, genes // CHUNKS), jnp.bfloat16)
    row = jax.ShapeDtypeStruct((genes // HALVES, cells), jnp.bfloat16)
    outs = pl.pallas_call(
        functools.partial(standardize_kernel, len(terms)),
        in_specs=[VMEM] * (3 + len(terms)),
        out_specs=[VMEM] * (CHUNKS + HALVES),
        out_shape=[block] * CHUNKS + [row] * HALVES,
        cost_estimate=pl.CostEstimate(
            flops=20 * cells * genes,
            bytes_accessed=8 * cells * genes,
            transcendentals=cells * genes,
        ),
        name="standardize",
    )(counts, gene_mean[None, :], gene_std[None, :], *terms)
    return outs[:CHUNKS], outs[CHUNKS:]


def line_steps(block, outer, inner):
    ups, downs = [block], [block]
    for h in range(1, outer):
        up = [
            (o * inner + i, (o + 1) * inner + i)
            for o in range(h - 1, outer - 1)
            for i in range(inner)
        ]
        down = [
            (o * inner + i, (o - 1) * inner + i)
            for o in range(1, outer - h + 1)
            for i in range(inner)
        ]
        ups.append(send(ups[-1], "gene", up))
        downs.append(send(downs[-1], "gene", down))
    return ups, downs


def pick_kernel(outer, place_ref, *refs):
    sources = refs[: 2 * outer - 1]
    outs = refs[2 * outer - 1 : 3 * outer - 1]
    sems = refs[3 * outer - 1]
    for j in range(outer):
        for k in range(2 * outer - 1):

            @pl.when(place_ref[j] == k)
            def _():
                pltpu.make_async_copy(sources[k], outs[j], sems.at[j]).start()

    for j in range(outer):
        pltpu.make_async_copy(sources[0], outs[j], sems.at[j]).wait()


def pick(place, ups, downs):
    outer = len(ups)
    sources = list(reversed(downs[1:])) + ups
    shape = jax.ShapeDtypeStruct(ups[0].shape, ups[0].dtype)
    size = ups[0].size * 2
    return pl.pallas_call(
        functools.partial(pick_kernel, outer),
        in_specs=[pl.BlockSpec(memory_space=pltpu.SMEM)]
        + [pl.BlockSpec(memory_space=pl.ANY)] * len(sources),
        out_specs=[pl.BlockSpec(memory_space=pl.ANY)] * outer,
        out_shape=[shape] * outer,
        scratch_shapes=[pltpu.SemaphoreType.DMA((outer,))],
        cost_estimate=pl.CostEstimate(
            flops=0, bytes_accessed=2 * outer * size, transcendentals=0
        ),
        name="pick_blocks",
    )(place, *sources)


def gram_kernel(groups, tiles, scale, place_ref, *refs):
    cols = refs[HALVES * groups : (HALVES + 1) * groups]
    out_ref = refs[-1]
    for half in range(HALVES):
        rows = refs[half * groups : (half + 1) * groups]

        @pl.when(pl.program_id(0) // tiles == half)
        def _():
            total = jnp.dot(
                rows[0][...], cols[0][...], preferred_element_type=jnp.float32
            )
            for j in range(1, groups):
                total += jnp.dot(
                    rows[j][...], cols[j][...], preferred_element_type=jnp.float32
                )
            out_ref[...] = total * scale


def gram_part(gram, column_block, rows, cols, shape, scale):
    groups = len(cols)
    height, depth = rows[0][0].shape
    width = cols[0].shape[1]
    tile = min(512, height)
    tiles = height // tile
    in_specs, operands = [], []
    for half in range(HALVES):
        at = functools.partial(
            lambda half, m, place: (jnp.clip(m - half * tiles, 0, tiles - 1), 0), half
        )
        in_specs += [pl.BlockSpec((tile, depth), at)] * groups
        operands += rows[half]
    in_specs += [pl.BlockSpec((depth, width), lambda m, place: (0, 0))] * groups
    operands += cols
    aliases = {}
    if gram is not None:
        aliases = {1 + len(operands): 0}
        in_specs.append(pl.BlockSpec(memory_space=pl.ANY))
        operands.append(gram)
    return pl.pallas_call(
        functools.partial(gram_kernel, groups, tiles, scale),
        grid_spec=pltpu.PrefetchScalarGridSpec(
            num_scalar_prefetch=1,
            grid=(HALVES * tiles,),
            in_specs=in_specs,
            out_specs=pl.BlockSpec((tile, width), lambda m, place: (m, place[0])),
        ),
        out_shape=jax.ShapeDtypeStruct(shape, jnp.float32),
        input_output_aliases=aliases,
        cost_estimate=pl.CostEstimate(
            flops=2 * groups * shape[0] * depth * width,
            bytes_accessed=4 * shape[0] * width
            + 2 * groups * depth * (shape[0] + width),
            transcendentals=0,
        ),
        name="gram_part",
    )(column_block, *operands)


def row_blocks(mine, groups):
    def cross(x, j):
        return send(x, "cell", [(c, c ^ j) for c in range(groups)])

    if groups != 4:
        return [[x] + [cross(x, j) for j in range(1, groups)] for x in mine]
    a, b = mine
    a1, a2, b1, b2 = cross(a, 1), cross(a, 2), cross(b, 1), cross(b, 2)
    return [[a, a1, a2, cross(a1, 2)], [b, b1, b2, cross(b2, 1)]]


def place_table(groups, outer, inner):
    table = np.zeros((groups, outer * inner, groups + inner), np.int32)
    for c in range(groups):
        for o in range(outer):
            for i in range(inner):
                line = [(c ^ j) for j in range(groups)]
                table[c, o * inner + i] = [outer - 1 + o - to for to in line] + [
                    (i + s) % inner for s in range(inner)
                ]
    return table


def shards(counts, gene_mean, gene_std):
    groups = lax.axis_size("cell")
    outer, inner = groups, lax.axis_size("gene") // groups
    cells, genes = counts.shape
    table = place_table(groups, outer, inner)
    place = jnp.asarray(table)[lax.axis_index("cell"), lax.axis_index("gene")]

    terms = library_terms(count_part(counts), outer, inner)
    blocks, mine = standardize(counts, terms, gene_mean, gene_std)
    rows = row_blocks(mine, groups)

    shape = (genes, genes * inner)
    scale = 1.0 / (cells * groups)
    gram = None
    for q in range(CHUNKS):
        ups, downs = line_steps(blocks[q], outer, inner)
        sends = pick(place[:groups], ups, downs)
        cols = [sends[0]] + [
            send(sends[j], "cell", [(c, c ^ j) for c in range(groups)])
            for j in range(1, groups)
        ]
        for s in range(inner):
            perm = [
                (o * inner + (i + s) % inner, o * inner + i)
                for o in range(outer)
                for i in range(inner)
            ]
            theirs = [send(x, "gene", perm) for x in cols] if s else cols
            column_block = place[groups + s :][:1] * CHUNKS + q
            gram = gram_part(gram, column_block, rows, theirs, shape, scale)
    return gram


def solution(mesh):
    placed = (P("cell", "gene"), P("gene"), P("gene"))
    return jax.shard_map(
        shards, mesh=mesh, in_specs=placed, out_specs=P("gene", "cell"), check_vma=False
    )
```

```python
import functools

import jax
import jax.numpy as jnp
import numpy as np
from jax import lax
from jax.experimental import pallas as pl
from jax.experimental.pallas import tpu as pltpu
from jax.sharding import PartitionSpec as P

CHUNKS = 4
HALVES = 2
STRIP = 128
VMEM = pl.BlockSpec(memory_space=pltpu.VMEM)
ANY = pl.BlockSpec(memory_space=pl.ANY)


def send(x, axis, pairs):
    return lax.ppermute(x, axis, pairs)


def count_kernel(counts_ref, out_ref):
    cells, genes = counts_ref.shape
    total = counts_ref[:, :STRIP]
    for at in range(STRIP, genes, STRIP):
        total += counts_ref[:, at : at + STRIP]
    summed = jnp.sum(total, axis=1, keepdims=True)
    flat = jnp.broadcast_to(summed, (cells, STRIP)).T
    out_ref[...] = flat[:8, :]


def count_part(counts):
    cells, genes = counts.shape
    return pl.pallas_call(
        count_kernel,
        in_specs=[VMEM],
        out_specs=VMEM,
        out_shape=jax.ShapeDtypeStruct((8, cells), jnp.float32),
        cost_estimate=pl.CostEstimate(
            flops=cells * genes, bytes_accessed=4 * cells * genes, transcendentals=0
        ),
        name="count_part",
    )(counts)


def library_terms(part, outer, inner):
    total = part
    for s in range(1, inner):
        total = total + send(
            part,
            "gene",
            [
                (o * inner + i, o * inner + (i + s) % inner)
                for o in range(outer)
                for i in range(inner)
            ],
        )
    terms = [total]
    for s in range(1, outer):
        terms.append(
            send(
                total,
                "gene",
                [
                    (o * inner + i, (o + s) % outer * inner + i)
                    for o in range(outer)
                    for i in range(inner)
                ],
            )
        )
    return terms


def standardize_kernel(terms, counts_ref, mean_ref, std_ref, *refs):
    cells, genes = counts_ref.shape
    sums, blocks, rows = (
        refs[:terms],
        refs[terms : terms + CHUNKS],
        refs[terms + CHUNKS :],
    )
    library = sums[0][:1, :]
    for ref in sums[1:]:
        library = library + ref[:1, :]
    factor = jnp.broadcast_to(10000.0 / library, (STRIP, cells)).T
    width, height = genes // CHUNKS, genes // HALVES
    for q in range(CHUNKS):
        half = q * width // height
        start = q * width - half * height

        @pl.loop(0, width // STRIP)
        def _(k):
            there = pl.multiple_of(k * STRIP, STRIP)
            at = pl.ds(q * width + there, STRIP)
            normal = jnp.log1p(counts_ref[:, at] * factor)
            spread = 1.0 / jnp.maximum(std_ref[:, at], 0.1)
            scaled = jnp.minimum((normal - mean_ref[:, at]) * spread, 10.0)
            blocks[q][:, pl.ds(there, STRIP)] = scaled.astype(jnp.bfloat16)
            rows[half][pl.ds(start + there, STRIP), :] = scaled.T.astype(jnp.bfloat16)


def standardize(counts, terms, gene_mean, gene_std):
    cells, genes = counts.shape
    block = jax.ShapeDtypeStruct((cells, genes // CHUNKS), jnp.bfloat16)
    row = jax.ShapeDtypeStruct((genes // HALVES, cells), jnp.bfloat16)
    outs = pl.pallas_call(
        functools.partial(standardize_kernel, len(terms)),
        in_specs=[VMEM] * (3 + len(terms)),
        out_specs=[VMEM] * (CHUNKS + HALVES),
        out_shape=[block] * CHUNKS + [row] * HALVES,
        cost_estimate=pl.CostEstimate(
            flops=20 * cells * genes,
            bytes_accessed=8 * cells * genes,
            transcendentals=cells * genes,
        ),
        name="standardize",
    )(counts, gene_mean[None, :], gene_std[None, :], *terms)
    return outs[:CHUNKS], outs[CHUNKS:]


def pick_kernel(places, depth, place_ref, source_ref, *refs):
    outs = refs[-places:]
    for j in range(places):
        at = pl.multiple_of(place_ref[j] * depth, depth)
        outs[j][...] = source_ref[pl.ds(at, depth), :]


def pick(place, line, groups, after):
    depth, width = line.shape[0] // groups, line.shape[1]
    return pl.pallas_call(
        functools.partial(pick_kernel, groups, depth),
        in_specs=[pl.BlockSpec(memory_space=pltpu.SMEM), VMEM] + [ANY] * len(after),
        out_specs=[VMEM] * groups,
        out_shape=[jax.ShapeDtypeStruct((depth, width), line.dtype)] * groups,
        cost_estimate=pl.CostEstimate(
            flops=0, bytes_accessed=2 * 2 * groups * depth * width, transcendentals=0
        ),
        name="pick_blocks",
    )(place, line, *after)


def stack_kernel(refs_in, axis, *refs):
    out_ref = refs[-1]
    size = refs[0].shape[axis]
    per_line = refs_in // HALVES if axis else refs_in
    for k in range(refs_in):
        if axis:
            high, wide = refs[0].shape
            line, at = k // per_line * high, k % per_line * wide
            out_ref[line : line + high, at : at + wide] = refs[k][...]
        else:
            out_ref[k * size : (k + 1) * size, :] = refs[k][...]


def stack(blocks, axis, after=()):
    high, wide = blocks[0].shape
    lines = HALVES if axis else len(blocks)
    shape = (lines * high, len(blocks) // lines * wide)
    return pl.pallas_call(
        functools.partial(stack_kernel, len(blocks), axis),
        in_specs=[VMEM] * len(blocks) + [ANY] * len(after),
        out_specs=VMEM,
        out_shape=jax.ShapeDtypeStruct(shape, blocks[0].dtype),
        cost_estimate=pl.CostEstimate(
            flops=0, bytes_accessed=4 * shape[0] * shape[1], transcendentals=0
        ),
        name="stack_blocks",
    )(*blocks, *after)


def gram_kernel(owner, start, scale, place_ref, rows_ref, cols_ref, *refs):
    out_ref, done_ref, tiles, sems = refs[-4:]
    tile, width = tiles.shape[1:]
    genes = rows_ref.shape[0]
    at = pl.multiple_of(place_ref[owner] * genes + start, STRIP)

    def copy(m):
        return pltpu.make_async_copy(
            tiles.at[m % 2],
            out_ref.at[pl.ds(m * tile, tile), pl.ds(at, width)],
            sems.at[m % 2],
        )

    count = genes // tile
    for m in range(count):
        if m >= 2:
            copy(m - 2).wait()
        total = jnp.dot(
            rows_ref[m * tile : (m + 1) * tile, :],
            cols_ref[...],
            preferred_element_type=jnp.float32,
        )
        tiles[m % 2] = total * scale
        copy(m).start()
    for m in range(max(count - 2, 0), count):
        copy(m).wait()
    done_ref[...] = jnp.zeros_like(done_ref)


def gram_part(gram, place, owner, start, rows, cols, shape, scale, after=()):
    genes, depth = rows.shape
    width = cols.shape[1]
    tile = min(512, genes)
    operands = [place, rows, cols, *after]
    in_specs = [pl.BlockSpec(memory_space=pltpu.SMEM), VMEM, VMEM] + [ANY] * len(after)
    aliases = {}
    if gram is not None:
        aliases = {len(operands): 0}
        in_specs.append(ANY)
        operands.append(gram)
    return pl.pallas_call(
        functools.partial(gram_kernel, owner, start, scale),
        in_specs=in_specs,
        out_specs=[ANY, VMEM],
        out_shape=[
            jax.ShapeDtypeStruct(shape, jnp.float32),
            jax.ShapeDtypeStruct((8, 128), jnp.float32),
        ],
        scratch_shapes=[
            pltpu.VMEM((2, tile, width), jnp.float32),
            pltpu.SemaphoreType.DMA((2,)),
        ],
        input_output_aliases=aliases,
        compiler_params=pltpu.CompilerParams(vmem_limit_bytes=24 * 2**20),
        cost_estimate=pl.CostEstimate(
            flops=2 * genes * depth * width,
            bytes_accessed=4 * genes * width,
            transcendentals=0,
        ),
        name="gram_part",
    )(*operands)


def row_blocks(mine, groups):
    def cross(x, j):
        return send(x, "cell", [(c, c ^ j) for c in range(groups)])

    if groups != 4:
        return [[x] + [cross(x, j) for j in range(1, groups)] for x in mine]
    a, b = mine
    a1, a2, b1, b2 = cross(a, 1), cross(a, 2), cross(b, 1), cross(b, 2)
    return [[a, a1, a2, cross(a1, 2)], [b, b1, b2, cross(b2, 1)]]


def place_table(groups, outer, inner):
    table = np.zeros((groups, outer * inner, groups + inner), np.int32)
    for c in range(groups):
        for o in range(outer):
            for i in range(inner):
                table[c, o * inner + i] = [c ^ j for j in range(groups)] + [
                    (i + s) % inner for s in range(inner)
                ]
    return table


def shards(counts, gene_mean, gene_std):
    groups = lax.axis_size("cell")
    outer, inner = groups, lax.axis_size("gene") // groups
    cells, genes = counts.shape
    table = place_table(groups, outer, inner)
    place = jnp.asarray(table)[lax.axis_index("cell"), lax.axis_index("gene")]

    terms = library_terms(count_part(counts), outer, inner)
    blocks, mine = standardize(counts, terms, gene_mean, gene_std)
    lines = [[o * inner + i for o in range(outer)] for i in range(inner)]
    gathered = [
        lax.all_gather(x, "gene", axis_index_groups=lines, axis=0, tiled=True)
        for x in blocks
    ]
    rows = row_blocks(mine, groups)
    deep = None

    shape = (genes, genes * inner)
    scale = 1.0 / (cells * groups)
    width = genes // CHUNKS
    across = [[(c, c ^ j) for c in range(groups)] for j in range(groups)]
    swap = [
        [
            (o * inner + (i + s) % inner, o * inner + i)
            for o in range(outer)
            for i in range(inner)
        ]
        for s in range(inner)
    ]
    gram, theirs, after = None, [], []
    for q in range(CHUNKS):
        sends = pick(place, gathered[q], groups, after)
        came = [sends[0]]
        came += [send(sends[j], "cell", across[j]) for j in range(1, groups)]
        if deep is None:
            deep = stack([x for half in rows for x in half], 1)
        for s, cols in theirs:
            gram, done = gram_part(
                gram, place, groups + s, (q - 1) * width, deep, cols, shape, scale, sends[:1]
            )
            after = [done]
        own = stack(came, 0, after)
        theirs = [(s, send(own, "gene", swap[s])) for s in range(1, inner)]
        gram, done = gram_part(
            gram, place, groups, q * width, deep, own, shape, scale
        )
        after = [done]
    for s, cols in theirs:
        gram, done = gram_part(
            gram, place, groups + s, (CHUNKS - 1) * width, deep, cols, shape, scale
        )
    return gram


def solution(mesh):
    placed = (P("cell", "gene"), P("gene"), P("gene"))
    return jax.shard_map(
        shards, mesh=mesh, in_specs=placed, out_specs=P("gene", "cell"), check_vma=False
    )
```

```python
import functools

import jax
import jax.numpy as jnp
import numpy as np
from jax import lax
from jax.experimental import pallas as pl
from jax.experimental.pallas import tpu as pltpu
from jax.sharding import PartitionSpec as P

STRIP = 128
SHARES = (6, 5, 5)
GATHERS = ((0, 1), (2,))
HALVES = 2
TILE = 1024
MIB = 2**20
SLACK = 8
VMEM = pl.BlockSpec(memory_space=pltpu.VMEM)
SMEM = pl.BlockSpec(memory_space=pltpu.SMEM)
ANY = pl.BlockSpec(memory_space=pl.ANY)


def send(x, axis, pairs):
    return lax.ppermute(x, axis, pairs)


def call(kernel, name, cost, vmem=8, **kwargs):
    flops, moved, transcendentals = cost
    return pl.pallas_call(
        kernel,
        name=name,
        cost_estimate=pl.CostEstimate(
            flops=flops // SLACK,
            bytes_accessed=moved // SLACK,
            transcendentals=transcendentals // SLACK,
        ),
        compiler_params=pltpu.CompilerParams(vmem_limit_bytes=vmem * MIB),
        **kwargs,
    )


def count_kernel(counts_ref, out_ref):
    cells, genes = counts_ref.shape
    total = counts_ref[:, :STRIP]
    for at in range(STRIP, genes, STRIP):
        total += counts_ref[:, at : at + STRIP]
    summed = jnp.sum(total, axis=1, keepdims=True)
    flat = jnp.broadcast_to(summed, (cells, STRIP)).T
    out_ref[...] = flat[:8, :]


def count_part(counts):
    cells, genes = counts.shape
    return call(
        count_kernel,
        "count_part",
        (cells * genes, 4 * cells * genes, 0),
        in_specs=[VMEM],
        out_specs=VMEM,
        out_shape=jax.ShapeDtypeStruct((8, cells), jnp.float32),
    )(counts)


def library_terms(part, size):
    terms, step = [part], 1
    while step < size:
        part = terms[0] if len(terms) == 1 else terms[0] + terms[1]
        terms = [part, send(part, "gene", [(g, g ^ step) for g in range(size)])]
        step *= 2
    return terms


def scaled_strip(counts_ref, mean_ref, std_ref, factor, at):
    normal = jnp.log1p(counts_ref[:, at] * factor)
    spread = 1.0 / jnp.maximum(std_ref[:, at], 0.1)
    return jnp.minimum((normal - mean_ref[:, at]) * spread, 10.0)


def cell_factor(sums, cells):
    library = sums[0][:1, :]
    for ref in sums[1:]:
        library = library + ref[:1, :]
    return jnp.broadcast_to(10000.0 / library, (STRIP, cells)).T


def block_kernel(terms, start, counts_ref, mean_ref, std_ref, *refs):
    factor = cell_factor(refs[:terms], counts_ref.shape[0])
    out_ref = refs[-1]

    @pl.loop(0, out_ref.shape[1] // STRIP)
    def _(k):
        there = pl.multiple_of(k * STRIP, STRIP)
        at = pl.ds(start + there, STRIP)
        scaled = scaled_strip(counts_ref, mean_ref, std_ref, factor, at)
        out_ref[:, pl.ds(there, STRIP)] = scaled.astype(jnp.bfloat16)


def rows_kernel(terms, counts_ref, mean_ref, std_ref, *refs):
    factor = cell_factor(refs[:terms], counts_ref.shape[0])
    outs = refs[-HALVES:]
    height = outs[0].shape[0]
    for half, out_ref in enumerate(outs):

        @pl.loop(0, height // STRIP)
        def _(k):
            there = pl.multiple_of(k * STRIP, STRIP)
            at = pl.ds(half * height + there, STRIP)
            scaled = scaled_strip(counts_ref, mean_ref, std_ref, factor, at)
            out_ref[pl.ds(there, STRIP), :] = scaled.T.astype(jnp.bfloat16)


def standardize(kernel, name, shape, pieces, counts, mean, std, terms, after=()):
    size = pieces * shape[0] * shape[1]
    return call(
        functools.partial(kernel, len(terms)),
        name,
        (20 * size, 6 * size, size),
        in_specs=[VMEM] * (3 + len(terms)) + [ANY] * len(after),
        out_specs=[VMEM] * pieces,
        out_shape=[jax.ShapeDtypeStruct(shape, jnp.bfloat16)] * pieces,
    )(counts, mean, std, *terms, *after)


def row_blocks(mine, groups):
    def cross(x, j):
        return send(x, "cell", [(c, c ^ j) for c in range(groups)])

    if groups != 4:
        return [[x] + [cross(x, j) for j in range(1, groups)] for x in mine]
    a, b = mine
    a1, b2, b1, a2 = cross(a, 1), cross(b, 2), cross(b, 1), cross(a, 2)
    return [[a, a1, a2, cross(a1, 2)], [b, b1, b2, cross(b2, 1)]]


def stack_kernel(lines, *refs):
    out_ref = refs[-1]
    high, wide = refs[0].shape
    for i, line in enumerate(lines):
        for j, k in enumerate(line):
            out_ref[i * high : (i + 1) * high, j * wide : (j + 1) * wide] = refs[k][...]


def stack(lines, after=()):
    blocks = [x for line in lines for x in line]
    count = len(lines[0])
    high, wide = blocks[0].shape
    shape = (len(lines) * high, count * wide)
    order = [[i * count + j for j in range(count)] for i in range(len(lines))]
    return call(
        functools.partial(stack_kernel, order),
        "stack_blocks",
        (0, 4 * shape[0] * shape[1], 0),
        vmem=4,
        in_specs=[VMEM] * len(blocks) + [ANY] * len(after),
        out_specs=VMEM,
        out_shape=jax.ShapeDtypeStruct(shape, blocks[0].dtype),
    )(*blocks, *after)


def pick_kernel(groups, start, place_ref, source_ref, *refs):
    outs, sems = refs[-groups - 1 : -1], refs[-1]
    depth, width = outs[0].shape
    copies = []
    for j in range(groups):
        line = pl.multiple_of(place_ref[j] * depth, depth)
        copies.append(
            pltpu.make_async_copy(
                source_ref.at[pl.ds(line, depth), start : start + width],
                outs[j],
                sems.at[j],
            )
        )
        copies[j].start()
    for copy in copies:
        copy.wait()


def pick(place, line, groups, start, width, after):
    depth = line.shape[0] // groups
    return call(
        functools.partial(pick_kernel, groups, start),
        "pick_blocks",
        (0, 4 * groups * depth * width, 0),
        vmem=4,
        in_specs=[SMEM, ANY] + [ANY] * len(after),
        out_specs=[VMEM] * groups,
        out_shape=[jax.ShapeDtypeStruct((depth, width), line.dtype)] * groups,
        scratch_shapes=[pltpu.SemaphoreType.DMA((groups,))],
    )(place, line, *after)


def gram_kernel(owner, start, scale, place_ref, rows_ref, cols_ref, *refs):
    out_ref, done_ref, tiles, sems = refs[-4:]
    tile, width = tiles.shape[1:]
    genes = rows_ref.shape[0]
    at = pl.multiple_of(place_ref[owner] * genes + start, STRIP)

    def give(m):
        return pltpu.make_async_copy(
            tiles.at[m % 2],
            out_ref.at[pl.ds(m * tile, tile), pl.ds(at, width)],
            sems.at[m % 2],
        )

    count = genes // tile
    for m in range(count):
        if m >= 2:
            give(m - 2).wait()
        total = jnp.dot(
            rows_ref[m * tile : (m + 1) * tile, :],
            cols_ref[...],
            preferred_element_type=jnp.float32,
        )
        tiles[m % 2] = total * scale
        give(m).start()
    for m in range(max(count - 2, 0), count):
        give(m).wait()
    done_ref[...] = jnp.zeros_like(done_ref)


def gram_part(gram, place, owner, start, rows, cols, shape, scale, after=()):
    genes, depth = rows.shape
    width = cols.shape[1]
    tile = min(TILE, genes)
    operands = [place, rows, cols, *after]
    in_specs = [SMEM, VMEM, VMEM] + [ANY] * len(after)
    aliases = {}
    if gram is not None:
        aliases = {len(operands): 0}
        in_specs.append(ANY)
        operands.append(gram)
    return call(
        functools.partial(gram_kernel, owner, start, scale),
        "gram_part",
        (2 * genes * depth * width, 4 * genes * width + 2 * genes * depth, 0),
        vmem=16,
        in_specs=in_specs,
        out_specs=[ANY, VMEM],
        out_shape=[
            jax.ShapeDtypeStruct(shape, jnp.float32),
            jax.ShapeDtypeStruct((8, 128), jnp.float32),
        ],
        scratch_shapes=[
            pltpu.VMEM((2, tile, width), jnp.float32),
            pltpu.SemaphoreType.DMA((2,)),
        ],
        input_output_aliases=aliases,
    )(*operands)


def place_table(groups, outer, inner):
    table = np.zeros((groups, outer * inner, groups + inner), np.int32)
    for c in range(groups):
        peers = [c ^ j for j in range(groups)]
        for o in range(outer):
            for i in range(inner):
                owners = [(i + s) % inner for s in range(inner)]
                table[c, o * inner + i] = peers + owners
    return table


def chunks(genes):
    units, spans, at = genes // STRIP, [], 0
    for share in SHARES[:-1]:
        size = max(1, units * share // sum(SHARES))
        spans.append((at * STRIP, size * STRIP))
        at += size
    return spans + [(at * STRIP, (units - at) * STRIP)]


def shards(counts, gene_mean, gene_std):
    groups = lax.axis_size("cell")
    outer, inner = groups, lax.axis_size("gene") // groups
    cells, genes = counts.shape
    table = place_table(groups, outer, inner)
    place = jnp.asarray(table)[lax.axis_index("cell"), lax.axis_index("gene")]
    given = counts, gene_mean[None, :], gene_std[None, :]
    given += (library_terms(count_part(counts), outer * inner),)

    spans, lines, after, mine = chunks(genes), [], [], None
    same = [[o * inner + i for o in range(outer)] for i in range(inner)]
    for members in GATHERS:
        first, width = spans[members[0]][0], sum(spans[q][1] for q in members)
        (block,) = standardize(
            lambda terms, *refs, first=first: block_kernel(terms, first, *refs),
            "standardize_block",
            (cells, width),
            1,
            *given,
            after,
        )
        line = lax.all_gather(
            block, "gene", axis_index_groups=same, axis=0, tiled=True
        )
        lines += [(line, spans[q][0] - first) for q in members]
        if mine is None:
            mine = standardize(
                rows_kernel,
                "standardize_rows",
                (genes // HALVES, cells),
                HALVES,
                *given,
                [block],
            )
            blocks = row_blocks(mine, groups)
            after = mine[:1]
    rows = stack(blocks, [block])

    shape = (genes, genes * inner)
    scale = 1.0 / (cells * groups)
    across = [[(c, c ^ j) for c in range(groups)] for j in range(groups)]
    swap = [
        [
            (o * inner + (i + s) % inner, o * inner + i)
            for o in range(outer)
            for i in range(inner)
        ]
        for s in range(inner)
    ]
    write = functools.partial(gram_part, shape=shape, scale=scale, rows=rows)
    gram, done, sent, arrived = None, rows, [], []

    def fetch(q):
        line, first = lines[q]
        sends = pick(place, line, groups, first, spans[q][1], [done] + sent[-1:])
        sent.append(sends[0])
        cols = [send(sends[j], "cell", across[j]) for j in range(1, groups)]
        arrived.append([sends[0]] + cols)

    fetch(0)
    owned = []
    for q, (start, _) in enumerate(spans):
        if q + 1 < len(spans):
            fetch(q + 1)
        own = stack([[x] for x in arrived[q]], owned[-1:] or sent[q + 1 : q + 2])
        theirs = [send(own, "gene", swap[s]) for s in range(1, inner)]
        for s, cols in enumerate([own] + theirs):
            after = sent[q + 1 : q + 2] if s == 0 else []
            gram, done = write(gram, place, groups + s, start, cols=cols, after=after)
            if s == 0:
                owned.append(done)
    return gram


def solution(mesh):
    placed = (P("cell", "gene"), P("gene"), P("gene"))
    return jax.shard_map(
        shards, mesh=mesh, in_specs=placed, out_specs=P("gene", "cell"), check_vma=False
    )
```

```python
import functools

import jax
import jax.numpy as jnp
import numpy as np
from jax import lax
from jax.experimental import pallas as pl
from jax.experimental.pallas import tpu as pltpu
from jax.sharding import PartitionSpec as P

STRIP = 128
SHARES = (3, 3, 2)
HALVES = 2
TILE = 1024
MIB = 2**20
SLACK = 8
VMEM = pl.BlockSpec(memory_space=pltpu.VMEM)
SMEM = pl.BlockSpec(memory_space=pltpu.SMEM)
ANY = pl.BlockSpec(memory_space=pl.ANY)


def send(x, axis, pairs):
    return lax.ppermute(x, axis, pairs)


def call(kernel, name, cost, vmem=8, **kwargs):
    flops, moved, transcendentals = cost
    return pl.pallas_call(
        kernel,
        name=name,
        cost_estimate=pl.CostEstimate(
            flops=flops // SLACK,
            bytes_accessed=moved // SLACK,
            transcendentals=transcendentals // SLACK,
        ),
        compiler_params=pltpu.CompilerParams(vmem_limit_bytes=vmem * MIB),
        **kwargs,
    )


def count_kernel(counts_ref, out_ref):
    cells, genes = counts_ref.shape
    total = counts_ref[:, :STRIP]
    for at in range(STRIP, genes, STRIP):
        total += counts_ref[:, at : at + STRIP]
    summed = jnp.sum(total, axis=1, keepdims=True)
    flat = jnp.broadcast_to(summed, (cells, STRIP)).T
    out_ref[...] = flat[:8, :]


def count_part(counts):
    cells, genes = counts.shape
    return call(
        count_kernel,
        "count_part",
        (cells * genes, 4 * cells * genes, 0),
        in_specs=[VMEM],
        out_specs=VMEM,
        out_shape=jax.ShapeDtypeStruct((8, cells), jnp.float32),
    )(counts)


def library_terms(part, size):
    terms, step = [part], 1
    while step < size:
        part = terms[0] if len(terms) == 1 else terms[0] + terms[1]
        terms = [part, send(part, "gene", [(g, g ^ step) for g in range(size)])]
        step *= 2
    return terms


def scaled_strip(counts_ref, mean_ref, std_ref, factor, at):
    normal = jnp.log1p(counts_ref[:, at] * factor)
    spread = 1.0 / jnp.maximum(std_ref[:, at], 0.1)
    return jnp.minimum((normal - mean_ref[:, at]) * spread, 10.0)


def cell_factor(sums, cells):
    library = sums[0][:1, :]
    for ref in sums[1:]:
        library = library + ref[:1, :]
    return jnp.broadcast_to(10000.0 / library, (STRIP, cells)).T


def block_kernel(terms, start, counts_ref, mean_ref, std_ref, *refs):
    factor = cell_factor(refs[:terms], counts_ref.shape[0])
    out_ref = refs[-1]

    @pl.loop(0, out_ref.shape[1] // STRIP)
    def _(k):
        there = pl.multiple_of(k * STRIP, STRIP)
        at = pl.ds(start + there, STRIP)
        scaled = scaled_strip(counts_ref, mean_ref, std_ref, factor, at)
        out_ref[:, pl.ds(there, STRIP)] = scaled.astype(jnp.bfloat16)


def rows_kernel(terms, counts_ref, mean_ref, std_ref, *refs):
    factor = cell_factor(refs[:terms], counts_ref.shape[0])
    outs = refs[-HALVES:]
    height = outs[0].shape[0]
    for half, out_ref in enumerate(outs):

        @pl.loop(0, height // STRIP)
        def _(k):
            there = pl.multiple_of(k * STRIP, STRIP)
            at = pl.ds(half * height + there, STRIP)
            scaled = scaled_strip(counts_ref, mean_ref, std_ref, factor, at)
            out_ref[pl.ds(there, STRIP), :] = scaled.T.astype(jnp.bfloat16)


def standardize(kernel, name, shape, pieces, counts, mean, std, terms, after=()):
    size = pieces * shape[0] * shape[1]
    return call(
        functools.partial(kernel, len(terms)),
        name,
        (20 * size, 6 * size, size),
        in_specs=[VMEM] * (3 + len(terms)) + [ANY] * len(after),
        out_specs=[VMEM] * pieces,
        out_shape=[jax.ShapeDtypeStruct(shape, jnp.bfloat16)] * pieces,
    )(counts, mean, std, *terms, *after)


def row_blocks(mine, groups):
    def cross(x, j):
        return send(x, "cell", [(c, c ^ j) for c in range(groups)])

    if groups != 4:
        return [[x] + [cross(x, j) for j in range(1, groups)] for x in mine]
    a, b = mine
    a1, b2, b1, a2 = cross(a, 1), cross(b, 2), cross(b, 1), cross(a, 2)
    return [[a, a1, a2, cross(a1, 2)], [b, b1, b2, cross(b2, 1)]]


def stack_kernel(lines, *refs):
    out_ref = refs[-1]
    high, wide = refs[0].shape
    for i, line in enumerate(lines):
        for j, k in enumerate(line):
            out_ref[i * high : (i + 1) * high, j * wide : (j + 1) * wide] = refs[k][...]


def stack(lines, after=()):
    blocks = [x for line in lines for x in line]
    count = len(lines[0])
    high, wide = blocks[0].shape
    shape = (len(lines) * high, count * wide)
    order = [[i * count + j for j in range(count)] for i in range(len(lines))]
    return call(
        functools.partial(stack_kernel, order),
        "stack_blocks",
        (0, 4 * shape[0] * shape[1], 0),
        vmem=4,
        in_specs=[VMEM] * len(blocks) + [ANY] * len(after),
        out_specs=VMEM,
        out_shape=jax.ShapeDtypeStruct(shape, blocks[0].dtype),
    )(*blocks, *after)


def line_pairs(outer, inner, moves):
    return [(a * inner + i, b * inner + i) for a, b in moves for i in range(inner)]


def line_gather(block, outer, inner, after):
    def move(x, moves):
        return send(x, "gene", line_pairs(outer, inner, moves))

    if outer == 4:
        near = move(block, [(0, 1), (1, 0), (2, 3), (3, 2)])
        both = stack([[block], [near]], after)
        across = move(both, [(1, 2), (2, 1)])
        ends = move(across, [(1, 0), (2, 3)])
        return both, [block, near, across, ends]
    ups, downs = [block], [block]
    for h in range(1, outer):
        ups.append(move(ups[-1], [(o, o + 1) for o in range(h - 1, outer - 1)]))
        downs.append(move(downs[-1], [(o, o - 1) for o in range(1, outer - h + 1)]))
    return block, [block] + ups[1:] + downs[1:]


def line_place(outer, at, wanted):
    if outer == 4:
        far = {0: (2, 3), 1: (2, 3), 2: (1, 0), 3: (1, 0)}[at]
        if wanted in far:
            return far.index(wanted) + (2 if at in (1, 2) else 4)
        return int(wanted != at)
    if wanted <= at:
        return at - wanted
    return outer - 1 + wanted - at


def pick_kernel(groups, arrays, place_ref, *refs):
    outs = refs[-groups:]
    depth = outs[0].shape[0]
    sources = [
        (ref, part * depth)
        for ref in refs[:arrays]
        for part in range(ref.shape[0] // depth)
    ]
    for j in range(groups):
        for k, (ref, line) in enumerate(sources):

            @pl.when(place_ref[groups + j] == k)
            def _():
                outs[j][...] = ref[line : line + depth, :]


def pick(place, arrays, groups, after):
    depth, width = arrays[0].shape
    return call(
        functools.partial(pick_kernel, groups, len(arrays)),
        "pick_blocks",
        (0, 4 * groups * depth * width, 0),
        vmem=4,
        in_specs=[SMEM] + [VMEM] * len(arrays) + [ANY] * len(after),
        out_specs=[VMEM] * groups,
        out_shape=[jax.ShapeDtypeStruct((depth, width), arrays[0].dtype)] * groups,
    )(place, *arrays, *after)


def gram_kernel(owner, start, scale, place_ref, rows_ref, cols_ref, *refs):
    out_ref, done_ref, tiles, sems = refs[-4:]
    tile, width = tiles.shape[1:]
    genes = rows_ref.shape[0]
    at = pl.multiple_of(place_ref[owner] * genes + start, STRIP)

    def give(m):
        return pltpu.make_async_copy(
            tiles.at[m % 2],
            out_ref.at[pl.ds(m * tile, tile), pl.ds(at, width)],
            sems.at[m % 2],
        )

    count = genes // tile
    for m in range(count):
        if m >= 2:
            give(m - 2).wait()
        total = jnp.dot(
            rows_ref[m * tile : (m + 1) * tile, :],
            cols_ref[...],
            preferred_element_type=jnp.float32,
        )
        tiles[m % 2] = total * scale
        give(m).start()
    for m in range(max(count - 2, 0), count):
        give(m).wait()
    done_ref[...] = jnp.zeros_like(done_ref)


def gram_part(gram, place, owner, start, rows, cols, shape, scale, after=()):
    genes, depth = rows.shape
    width = cols.shape[1]
    tile = min(TILE, genes)
    operands = [place, rows, cols, *after]
    in_specs = [SMEM, VMEM, VMEM] + [ANY] * len(after)
    aliases = {}
    if gram is not None:
        aliases = {len(operands): 0}
        in_specs.append(ANY)
        operands.append(gram)
    return call(
        functools.partial(gram_kernel, owner, start, scale),
        "gram_part",
        (2 * genes * depth * width, 4 * genes * width + 2 * genes * depth, 0),
        vmem=16,
        in_specs=in_specs,
        out_specs=[ANY, VMEM],
        out_shape=[
            jax.ShapeDtypeStruct(shape, jnp.float32),
            jax.ShapeDtypeStruct((8, 128), jnp.float32),
        ],
        scratch_shapes=[
            pltpu.VMEM((2, tile, width), jnp.float32),
            pltpu.SemaphoreType.DMA((2,)),
        ],
        input_output_aliases=aliases,
    )(*operands)


def place_table(groups, outer, inner):
    table = np.zeros((groups, outer * inner, 2 * groups + inner), np.int32)
    for c in range(groups):
        peers = [c ^ j for j in range(groups)]
        for o in range(outer):
            line = [line_place(outer, o, to) for to in peers]
            for i in range(inner):
                owners = [(i + s) % inner for s in range(inner)]
                table[c, o * inner + i] = peers + line + owners
    return table


def chunks(genes):
    units, spans, at = genes // STRIP, [], 0
    for share in SHARES[:-1]:
        size = max(1, units * share // sum(SHARES))
        spans.append((at * STRIP, size * STRIP))
        at += size
    return spans + [(at * STRIP, (units - at) * STRIP)]


def shards(counts, gene_mean, gene_std):
    groups = lax.axis_size("cell")
    outer, inner = groups, lax.axis_size("gene") // groups
    cells, genes = counts.shape
    table = place_table(groups, outer, inner)
    place = jnp.asarray(table)[lax.axis_index("cell"), lax.axis_index("gene")]
    given = counts, gene_mean[None, :], gene_std[None, :]
    given += (library_terms(count_part(counts), outer * inner),)

    spans, lines, boths, after, mine = chunks(genes), [], [], [], None
    for start, width in spans:
        (block,) = standardize(
            lambda terms, *refs, start=start: block_kernel(terms, start, *refs),
            "standardize_block",
            (cells, width),
            1,
            *given,
            after,
        )
        both, arrays = line_gather(block, outer, inner, boths[-1:])
        lines.append(arrays)
        boths.append(both)
        if mine is None:
            mine = standardize(
                rows_kernel,
                "standardize_rows",
                (genes // HALVES, cells),
                HALVES,
                *given,
                [block],
            )
            blocks = row_blocks(mine, groups)
        after = [block, mine[0]]
    rows = stack(blocks)

    shape = (genes, genes * inner)
    scale = 1.0 / (cells * groups)
    across = [[(c, c ^ j) for c in range(groups)] for j in range(groups)]
    swap = [
        [
            (o * inner + (i + s) % inner, o * inner + i)
            for o in range(outer)
            for i in range(inner)
        ]
        for s in range(inner)
    ]
    write = functools.partial(gram_part, shape=shape, scale=scale, rows=rows)
    gram, done, sent, arrived = None, rows, [], []

    def fetch(q):
        ahead = lines[q + 1][2:3] if q + 1 < len(spans) else []
        sends = pick(place, lines[q], groups, [done] + sent[-1:] + boths[-1:] + ahead)
        sent.append(sends[0])
        cols = [send(sends[j], "cell", across[j]) for j in range(1, groups)]
        arrived.append([sends[0]] + cols)

    fetch(0)
    owned = []
    for q, (start, _) in enumerate(spans):
        if q + 1 < len(spans):
            fetch(q + 1)
        own = stack([[x] for x in arrived[q]], owned[-1:] or sent[q + 1 : q + 2])
        theirs = [send(own, "gene", swap[s]) for s in range(1, inner)]
        for s, cols in enumerate([own] + theirs):
            after = sent[q + 1 : q + 2] if s == 0 else []
            gram, done = write(gram, place, 2 * groups + s, start, cols=cols, after=after)
            if s == 0:
                owned.append(done)
    return gram


def solution(mesh):
    placed = (P("cell", "gene"), P("gene"), P("gene"))
    return jax.shard_map(
        shards, mesh=mesh, in_specs=placed, out_specs=P("gene", "cell"), check_vma=False
    )
```

```python
import functools

import jax
import jax.numpy as jnp
from jax import lax
from jax.experimental import pallas as pl
from jax.experimental.pallas import tpu as pltpu
from jax.sharding import PartitionSpec as P

STRIP = 128
SHARES = (3, 3, 2)
TILE = 512
MIB = 2**20
SLACK = 8
VMEM = pl.BlockSpec(memory_space=pltpu.VMEM)
ANY = pl.BlockSpec(memory_space=pl.ANY)


def send(x, axis, pairs):
    return lax.ppermute(x, axis, pairs)


def call(kernel, name, cost, vmem=8, **kwargs):
    flops, moved, transcendentals = cost
    return pl.pallas_call(
        kernel,
        name=name,
        cost_estimate=pl.CostEstimate(
            flops=flops // SLACK,
            bytes_accessed=moved // SLACK,
            transcendentals=transcendentals // SLACK,
        ),
        compiler_params=pltpu.CompilerParams(vmem_limit_bytes=vmem * MIB),
        **kwargs,
    )


def count_kernel(counts_ref, mean_ref, std_ref, out_ref, genes_ref):
    cells, genes = counts_ref.shape
    total = counts_ref[:, :STRIP]
    for at in range(STRIP, genes, STRIP):
        total += counts_ref[:, at : at + STRIP]
    summed = jnp.sum(total, axis=1, keepdims=True)
    flat = jnp.broadcast_to(summed, (cells, STRIP)).T
    out_ref[...] = flat[:8, :]
    genes_ref[0:1, :] = mean_ref[...]
    genes_ref[1:2, :] = 1.0 / jnp.maximum(std_ref[...], 0.1)


def count_part(counts, mean, std):
    cells, genes = counts.shape
    return call(
        count_kernel,
        "count_part",
        (cells * genes, 4 * cells * genes, 0),
        vmem=4,
        in_specs=[VMEM] * 3,
        out_specs=[VMEM] * 2,
        out_shape=[
            jax.ShapeDtypeStruct((8, cells), jnp.float32),
            jax.ShapeDtypeStruct((8, genes), jnp.float32),
        ],
    )(counts, mean, std)


def add_kernel(a_ref, b_ref, out_ref):
    out_ref[...] = a_ref[...] + b_ref[...]


def add(a, b):
    return call(
        add_kernel,
        "add_terms",
        (a.size, 12 * a.size, 0),
        vmem=1,
        in_specs=[VMEM] * 2,
        out_specs=VMEM,
        out_shape=jax.ShapeDtypeStruct(a.shape, a.dtype),
    )(a, b)


def library_terms(part, size):
    terms, step = [part], 1
    while step < size:
        part = terms[0] if len(terms) == 1 else add(*terms)
        terms = [part, send(part, "gene", [(g, g ^ step) for g in range(size)])]
        step *= 2
    return terms


def scaled_strip(counts_ref, genes_ref, factor, at):
    normal = jnp.log1p(counts_ref[:, at] * factor)
    return jnp.minimum((normal - genes_ref[0:1, at]) * genes_ref[1:2, at], 10.0)


def cell_factor(sums, cells):
    library = sums[0][:1, :]
    for ref in sums[1:]:
        library = library + ref[:1, :]
    return jnp.broadcast_to(10000.0 / library, (STRIP, cells)).T


def block_kernel(terms, start, counts_ref, genes_ref, *refs):
    factor = cell_factor(refs[:terms], counts_ref.shape[0])
    out_ref = refs[-1]

    @pl.loop(0, out_ref.shape[1] // STRIP)
    def _(k):
        there = pl.multiple_of(k * STRIP, STRIP)
        at = pl.ds(start + there, STRIP)
        scaled = scaled_strip(counts_ref, genes_ref, factor, at)
        out_ref[:, pl.ds(there, STRIP)] = scaled.astype(jnp.bfloat16)


def rows_kernel(terms, counts_ref, genes_ref, *refs):
    factor = cell_factor(refs[:terms], counts_ref.shape[0])
    out_ref = refs[-1]

    @pl.loop(0, counts_ref.shape[1] // STRIP)
    def _(k):
        at = pl.ds(pl.multiple_of(k * STRIP, STRIP), STRIP)
        scaled = scaled_strip(counts_ref, genes_ref, factor, at)
        out_ref[at, :] = scaled.T.astype(jnp.bfloat16)


def standardize(kernel, name, shape, pieces, counts, scales, terms, after=()):
    size = pieces * shape[0] * shape[1]
    return call(
        functools.partial(kernel, len(terms)),
        name,
        (20 * size, 6 * size, size),
        in_specs=[VMEM] * (2 + len(terms)) + [ANY] * len(after),
        out_specs=[VMEM] * pieces,
        out_shape=[jax.ShapeDtypeStruct(shape, jnp.bfloat16)] * pieces,
    )(counts, scales, *terms, *after)


def split_kernel(one_ref, two_ref, *refs):
    top_ref, low_ref = refs[-2:]
    half = top_ref.shape[0]
    top_ref[...] = one_ref[:half, :]
    low_ref[...] = two_ref[half:, :]


def row_blocks(mine, groups, after):
    def cross(x, j):
        return send(x, "cell", [(c, c ^ j) for c in range(groups)])

    if groups != 4:
        return [[mine]] + [[cross(mine, j)] for j in range(1, groups)]
    one, two = cross(mine, 1), cross(mine, 2)
    half = jax.ShapeDtypeStruct((mine.shape[0] // 2, mine.shape[1]), mine.dtype)
    top, low = call(
        split_kernel,
        "split_rows",
        (0, 4 * mine.size, 0),
        vmem=4,
        in_specs=[VMEM] * 2 + [ANY] * len(after),
        out_specs=[VMEM] * 2,
        out_shape=[half] * 2,
    )(one, two, *after)
    return [[mine], [one], [two], [cross(top, 2), cross(low, 1)]]


def stack_kernel(places, *refs):
    out_ref = refs[-1]
    for ref, (line, at) in zip(refs, places):
        high, wide = ref.shape
        out_ref[line : line + high, at : at + wide] = ref[...]


def stack(columns, after=()):
    places, blocks, at = [], [], 0
    for column in columns:
        line = 0
        for x in column:
            places.append((line, at))
            blocks.append(x)
            line += x.shape[0]
        at += column[0].shape[1]
    return call(
        functools.partial(stack_kernel, places),
        "stack_blocks",
        (0, 4 * line * at, 0),
        vmem=4,
        in_specs=[VMEM] * len(blocks) + [ANY] * len(after),
        out_specs=VMEM,
        out_shape=jax.ShapeDtypeStruct((line, at), blocks[0].dtype),
    )(*blocks, *after)


def line_pairs(outer, inner, moves):
    return [(a * inner + i, b * inner + i) for a, b in moves for i in range(inner)]


def line_gather(block, outer, inner, after):
    def move(x, moves):
        return send(x, "gene", line_pairs(outer, inner, moves))

    if outer == 4:
        near = move(block, [(0, 1), (1, 0), (2, 3), (3, 2)])
        both = stack([[block, near]], after)
        across = move(both, [(1, 2), (2, 1)])
        ends = move(across, [(1, 0), (2, 3)])
        return both, [block, near, across, ends]
    ups, downs = [block], [block]
    for h in range(1, outer):
        ups.append(move(ups[-1], [(o, o + 1) for o in range(h - 1, outer - 1)]))
        downs.append(move(downs[-1], [(o, o - 1) for o in range(1, outer - h + 1)]))
    return block, [block] + ups[1:] + downs[1:]


def line_place(outer, at, wanted):
    if outer == 4:
        far = {0: (2, 3), 1: (2, 3), 2: (1, 0), 3: (1, 0)}[at]
        if wanted in far:
            return far.index(wanted) + (2 if at in (1, 2) else 4)
        return int(wanted != at)
    if wanted <= at:
        return at - wanted
    return outer - 1 + wanted - at


def pick_kernel(groups, outer, inner, arrays, *refs):
    outs = refs[-groups:]
    depth = outs[0].shape[0]
    sources = [
        (ref, part * depth)
        for ref in refs[:arrays]
        for part in range(ref.shape[0] // depth)
    ]
    cell_at = lax.axis_index("cell")
    line_at = lax.div(lax.axis_index("gene"), jnp.int32(inner))
    pairs = [(o, to) for o in range(outer) for to in range(outer)]
    for j in range(groups):
        here = line_at * outer + lax.bitwise_xor(cell_at, jnp.int32(j))
        for k, (ref, line) in enumerate(sources):
            found = [o * outer + to for o, to in pairs if line_place(outer, o, to) == k]
            match = functools.reduce(jnp.logical_or, [here == x for x in found])

            @pl.when(match)
            def _():
                outs[j][...] = ref[line : line + depth, :]


def pick(arrays, outer, inner, after):
    depth, width = arrays[0].shape
    return call(
        functools.partial(pick_kernel, outer, outer, inner, len(arrays)),
        "pick_blocks",
        (0, 4 * outer * depth * width, 0),
        vmem=4,
        in_specs=[VMEM] * len(arrays) + [ANY] * len(after),
        out_specs=[VMEM] * outer,
        out_shape=[jax.ShapeDtypeStruct((depth, width), arrays[0].dtype)] * outer,
    )(*arrays, *after)


def gram_kernel(inner, step, start, scale, rows_ref, cols_ref, *refs):
    out_ref, done_ref, tiles, sems = refs[-4:]
    tile, width = tiles.shape[1:]
    genes = rows_ref.shape[0]
    owner = lax.rem(lax.axis_index("gene") + step, jnp.int32(inner))
    at = pl.multiple_of(owner * genes + start, STRIP)

    def give(m):
        return pltpu.make_async_copy(
            tiles.at[m % 2],
            out_ref.at[pl.ds(m * tile, tile), pl.ds(at, width)],
            sems.at[m % 2],
        )

    count = genes // tile
    for m in range(count):
        if m >= 2:
            give(m - 2).wait()
        total = jnp.dot(
            rows_ref[m * tile : (m + 1) * tile, :],
            cols_ref[...],
            preferred_element_type=jnp.float32,
        )
        tiles[m % 2] = total * scale
        give(m).start()
    for m in range(max(count - 2, 0), count):
        give(m).wait()
    done_ref[...] = jnp.zeros_like(done_ref)


def gram_part(gram, step, start, cols, rows, shape, scale, after=()):
    genes, depth = rows.shape
    width = cols.shape[1]
    tile = min(TILE, genes)
    inner = shape[1] // genes
    operands = [rows, cols, *after]
    in_specs = [VMEM, VMEM] + [ANY] * len(after)
    aliases = {}
    if gram is not None:
        aliases = {len(operands): 0}
        in_specs.append(ANY)
        operands.append(gram)
    return call(
        functools.partial(gram_kernel, inner, step, start, scale),
        "gram_part",
        (2 * genes * depth * width, 4 * genes * width + 2 * genes * depth, 0),
        vmem=16,
        in_specs=in_specs,
        out_specs=[ANY, VMEM],
        out_shape=[
            jax.ShapeDtypeStruct(shape, jnp.float32),
            jax.ShapeDtypeStruct((8, 128), jnp.float32),
        ],
        scratch_shapes=[
            pltpu.VMEM((2, tile, width), jnp.float32),
            pltpu.SemaphoreType.DMA((2,)),
        ],
        input_output_aliases=aliases,
    )(*operands)


def chunks(genes):
    units, spans, at = genes // STRIP, [], 0
    for share in SHARES[:-1]:
        size = max(1, units * share // sum(SHARES))
        spans.append((at * STRIP, size * STRIP))
        at += size
    return spans + [(at * STRIP, (units - at) * STRIP)]


def shards(counts, gene_mean, gene_std):
    groups = lax.axis_size("cell")
    outer, inner = groups, lax.axis_size("gene") // groups
    cells, genes = counts.shape
    part, scales = count_part(counts, gene_mean[None, :], gene_std[None, :])
    given = counts, scales, library_terms(part, outer * inner)

    spans, lines, boths, mine = chunks(genes), [], [], None
    for start, width in spans:
        (block,) = standardize(
            lambda terms, *refs, start=start: block_kernel(terms, start, *refs),
            "standardize_block",
            (cells, width),
            1,
            *given,
            [] if mine is None else [mine] + boths[1:],
        )
        both, arrays = line_gather(block, outer, inner, boths[-1:])
        lines.append(arrays)
        boths.append(both)
        if mine is None:
            (mine,) = standardize(
                rows_kernel, "standardize_rows", (genes, cells), 1, *given, [block]
            )
    rows = stack(row_blocks(mine, groups, boths[1:2]))

    shape = (genes, genes * inner)
    scale = 1.0 / (cells * groups)
    across = [[(c, c ^ j) for c in range(groups)] for j in range(groups)]
    swap = [
        [
            (o * inner + (i + s) % inner, o * inner + i)
            for o in range(outer)
            for i in range(inner)
        ]
        for s in range(inner)
    ]
    write = functools.partial(gram_part, rows=rows, shape=shape, scale=scale)
    gram, done, sent, arrived = None, rows, [], []

    def fetch(q):
        ahead = lines[q + 1][2:3] if q + 1 < len(spans) else []
        sends = pick(lines[q], outer, inner, [done] + sent[-1:] + boths[-1:] + ahead)
        sent.append(sends[0])
        cols = [send(sends[j], "cell", across[j]) for j in range(1, groups)]
        arrived.append([sends[0]] + cols)

    fetch(0)
    for q, (start, _) in enumerate(spans):
        if q + 1 < len(spans):
            fetch(q + 1)
        own = stack([arrived[q]], [done] if q else sent[q + 1 : q + 2])
        theirs = [send(own, "gene", swap[s]) for s in range(1, inner)]
        for s, cols in enumerate([own] + theirs):
            after = sent[q + 1 : q + 2]
            if s > 0:
                after = [arrays[-1] for arrays in lines[q + 2 : q + 3]]
            gram, done = write(gram, s, start, cols, after=after)
    return gram


def solution(mesh):
    placed = (P("cell", "gene"), P("gene"), P("gene"))
    return jax.shard_map(
        shards, mesh=mesh, in_specs=placed, out_specs=P("gene", "cell"), check_vma=False
    )
```

```python
import functools

import jax
import jax.numpy as jnp
from jax import lax
from jax.experimental import pallas as pl
from jax.experimental.pallas import tpu as pltpu
from jax.sharding import PartitionSpec as P

STRIP = 128
SHARES = (3, 3, 2)
COLUMNS = 256
MIB = 2**20
SLACK = 8
VMEM = pl.BlockSpec(memory_space=pltpu.VMEM)
ANY = pl.BlockSpec(memory_space=pl.ANY)


def send(x, axis, pairs):
    return lax.ppermute(x, axis, pairs)


def call(kernel, name, cost, vmem=8, **kwargs):
    flops, moved, transcendentals = cost
    return pl.pallas_call(
        kernel,
        name=name,
        cost_estimate=pl.CostEstimate(
            flops=flops // SLACK,
            bytes_accessed=moved // SLACK,
            transcendentals=transcendentals // SLACK,
        ),
        compiler_params=pltpu.CompilerParams(vmem_limit_bytes=vmem * MIB),
        **kwargs,
    )


def count_kernel(counts_ref, out_ref, held_ref):
    cells, genes = counts_ref.shape
    total = jnp.zeros((cells, STRIP), jnp.float32)
    for at in range(0, genes, STRIP):
        strip = counts_ref[:, at : at + STRIP]
        held_ref[:, at : at + STRIP] = strip
        total += strip
    summed = jnp.sum(total, axis=1, keepdims=True)
    flat = jnp.broadcast_to(summed, (cells, STRIP)).T
    out_ref[...] = flat[:8, :]


def count_part(counts):
    cells, genes = counts.shape
    return call(
        count_kernel,
        "count_part",
        (cells * genes, 8 * cells * genes, 0),
        vmem=4,
        in_specs=[VMEM],
        out_specs=[VMEM] * 2,
        out_shape=[
            jax.ShapeDtypeStruct((8, cells), jnp.float32),
            jax.ShapeDtypeStruct(counts.shape, jnp.float32),
        ],
    )(counts)


def scales_kernel(mean_ref, std_ref, *refs):
    out_ref = refs[-1]
    out_ref[0:1, :] = mean_ref[...]
    out_ref[8:9, :] = 1.0 / jnp.maximum(std_ref[...], 0.1)


def gene_scales(mean, std, after):
    genes = mean.shape[1]
    return call(
        scales_kernel,
        "gene_scales",
        (2 * genes, 72 * genes, 0),
        vmem=1,
        in_specs=[VMEM] * 2 + [ANY] * len(after),
        out_specs=VMEM,
        out_shape=jax.ShapeDtypeStruct((16, genes), jnp.float32),
    )(mean, std, *after)


def add_kernel(a_ref, b_ref, out_ref):
    out_ref[...] = a_ref[...] + b_ref[...]


def add(a, b):
    return call(
        add_kernel,
        "add_terms",
        (a.size, 12 * a.size, 0),
        vmem=1,
        in_specs=[VMEM] * 2,
        out_specs=VMEM,
        out_shape=jax.ShapeDtypeStruct(a.shape, a.dtype),
    )(a, b)


def library_terms(part, size):
    terms, step = [part], 1
    while step < size:
        part = terms[0] if len(terms) == 1 else add(*terms)
        terms = [part, send(part, "gene", [(g, g ^ step) for g in range(size)])]
        step *= 2
    return terms


def scaled_strip(counts_ref, genes_ref, factor, at):
    normal = jnp.log1p(counts_ref[:, at] * factor)
    return jnp.minimum((normal - genes_ref[0:1, at]) * genes_ref[8:9, at], 10.0)


def cell_factor(sums, cells):
    library = sums[0][:1, :]
    for ref in sums[1:]:
        library = library + ref[:1, :]
    return jnp.broadcast_to(10000.0 / library, (STRIP, cells)).T


def block_kernel(terms, start, counts_ref, genes_ref, *refs):
    factor = cell_factor(refs[:terms], counts_ref.shape[0])
    out_ref = refs[-1]

    @pl.loop(0, out_ref.shape[1] // STRIP)
    def _(k):
        there = pl.multiple_of(k * STRIP, STRIP)
        at = pl.ds(start + there, STRIP)
        scaled = scaled_strip(counts_ref, genes_ref, factor, at)
        out_ref[:, pl.ds(there, STRIP)] = scaled.astype(jnp.bfloat16)


def rows_kernel(terms, counts_ref, genes_ref, *refs):
    factor = cell_factor(refs[:terms], counts_ref.shape[0])
    out_ref = refs[-1]

    @pl.loop(0, counts_ref.shape[1] // STRIP)
    def _(k):
        at = pl.ds(pl.multiple_of(k * STRIP, STRIP), STRIP)
        scaled = scaled_strip(counts_ref, genes_ref, factor, at)
        out_ref[at, :] = scaled.T.astype(jnp.bfloat16)


def standardize(kernel, name, shape, pieces, counts, scales, terms, after=()):
    size = pieces * shape[0] * shape[1]
    return call(
        functools.partial(kernel, len(terms)),
        name,
        (20 * size, 6 * size, size),
        in_specs=[VMEM] * (2 + len(terms)) + [ANY] * len(after),
        out_specs=[VMEM] * pieces,
        out_shape=[jax.ShapeDtypeStruct(shape, jnp.bfloat16)] * pieces,
    )(counts, scales, *terms, *after)


def split_kernel(one_ref, two_ref, *refs):
    top_ref, low_ref = refs[-2:]
    half = top_ref.shape[0]
    top_ref[...] = one_ref[:half, :]
    low_ref[...] = two_ref[half:, :]


def row_blocks(mine, groups, after):
    def cross(x, j):
        return send(x, "cell", [(c, c ^ j) for c in range(groups)])

    if groups != 4:
        return [[mine]] + [[cross(mine, j)] for j in range(1, groups)]
    one, two = cross(mine, 1), cross(mine, 2)
    half = jax.ShapeDtypeStruct((mine.shape[0] // 2, mine.shape[1]), mine.dtype)
    top, low = call(
        split_kernel,
        "split_rows",
        (0, 4 * mine.size, 0),
        vmem=4,
        in_specs=[VMEM] * 2 + [ANY] * len(after),
        out_specs=[VMEM] * 2,
        out_shape=[half] * 2,
    )(one, two, *after)
    return [[mine], [one], [two], [cross(top, 2), cross(low, 1)]]


def stack_kernel(places, *refs):
    out_ref = refs[-1]
    for ref, (line, at) in zip(refs, places):
        high, wide = ref.shape
        out_ref[line : line + high, at : at + wide] = ref[...]


def stack(columns, after=()):
    places, blocks, at = [], [], 0
    for column in columns:
        line = 0
        for x in column:
            places.append((line, at))
            blocks.append(x)
            line += x.shape[0]
        at += column[0].shape[1]
    return call(
        functools.partial(stack_kernel, places),
        "stack_blocks",
        (0, 4 * line * at, 0),
        vmem=4,
        in_specs=[VMEM] * len(blocks) + [ANY] * len(after),
        out_specs=VMEM,
        out_shape=jax.ShapeDtypeStruct((line, at), blocks[0].dtype),
    )(*blocks, *after)


def line_pairs(outer, inner, moves):
    return [(a * inner + i, b * inner + i) for a, b in moves for i in range(inner)]


def line_move(x, outer, inner, moves):
    return send(x, "gene", line_pairs(outer, inner, moves))


def line_near(block, outer, inner):
    if outer == 4:
        return line_move(block, outer, inner, [(0, 1), (1, 0), (2, 3), (3, 2)])
    return line_move(block, outer, inner, [(o, o + 1) for o in range(outer - 1)])


def line_gather(block, near, outer, inner, after):
    def move(x, moves):
        return line_move(x, outer, inner, moves)

    if outer == 4:
        both = stack([[block, near]], after)
        across = move(both, [(1, 2), (2, 1)])
        ends = move(across, [(1, 0), (2, 3)])
        return both, [block, near, across, ends]
    ups, downs = [block, near], [block]
    for h in range(1, outer):
        if h > 1:
            ups.append(move(ups[-1], [(o, o + 1) for o in range(h - 1, outer - 1)]))
        downs.append(move(downs[-1], [(o, o - 1) for o in range(1, outer - h + 1)]))
    return block, [block] + ups[1:] + downs[1:]


def line_place(outer, at, wanted):
    if outer == 4:
        far = {0: (2, 3), 1: (2, 3), 2: (1, 0), 3: (1, 0)}[at]
        if wanted in far:
            return far.index(wanted) + (2 if at in (1, 2) else 4)
        return int(wanted != at)
    if wanted <= at:
        return at - wanted
    return outer - 1 + wanted - at


def pick_kernel(groups, outer, inner, arrays, *refs):
    outs = refs[-groups:]
    depth = outs[0].shape[0]
    sources = [
        (ref, part * depth)
        for ref in refs[:arrays]
        for part in range(ref.shape[0] // depth)
    ]
    cell_at = lax.axis_index("cell")
    line_at = lax.div(lax.axis_index("gene"), jnp.int32(inner))
    pairs = [(o, to) for o in range(outer) for to in range(outer)]
    for j in range(groups):
        here = line_at * outer + lax.bitwise_xor(cell_at, jnp.int32(j))
        for k, (ref, line) in enumerate(sources):
            found = [o * outer + to for o, to in pairs if line_place(outer, o, to) == k]
            match = functools.reduce(jnp.logical_or, [here == x for x in found])

            @pl.when(match)
            def _():
                outs[j][...] = ref[line : line + depth, :]


def pick(arrays, outer, inner, after):
    depth, width = arrays[0].shape
    return call(
        functools.partial(pick_kernel, outer, outer, inner, len(arrays)),
        "pick_blocks",
        (0, 4 * outer * depth * width, 0),
        vmem=4,
        in_specs=[VMEM] * len(arrays) + [ANY] * len(after),
        out_specs=[VMEM] * outer,
        out_shape=[jax.ShapeDtypeStruct((depth, width), arrays[0].dtype)] * outer,
    )(*arrays, *after)


def gram_kernel(inner, step, start, scale, rows_ref, cols_ref, *refs):
    out_ref, done_ref, tiles, sems = refs[-4:]
    genes, width = tiles.shape[1:]
    owner = lax.rem(lax.axis_index("gene") + step, jnp.int32(inner))
    at = pl.multiple_of(owner * genes + start, STRIP)

    def give(n):
        return pltpu.make_async_copy(
            tiles.at[n % 2],
            out_ref.at[:, pl.ds(at + n * width, width)],
            sems.at[n % 2],
        )

    count = cols_ref.shape[1] // width
    for n in range(count):
        if n >= 2:
            give(n - 2).wait()
        total = jnp.dot(
            rows_ref[...],
            cols_ref[:, n * width : (n + 1) * width],
            preferred_element_type=jnp.float32,
        )
        tiles[n % 2] = total * scale
        give(n).start()
    for n in range(max(count - 2, 0), count):
        give(n).wait()
    done_ref[...] = jnp.zeros_like(done_ref)


def gram_part(gram, step, start, cols, rows, shape, scale, after=()):
    genes, depth = rows.shape
    width = cols.shape[1]
    tile = COLUMNS if width % COLUMNS == 0 else STRIP
    inner = shape[1] // genes
    operands = [rows, cols, *after]
    in_specs = [VMEM, VMEM] + [ANY] * len(after)
    aliases = {}
    if gram is not None:
        aliases = {len(operands): 0}
        in_specs.append(ANY)
        operands.append(gram)
    return call(
        functools.partial(gram_kernel, inner, step, start, scale),
        "gram_part",
        (2 * genes * depth * width, 4 * genes * width + 2 * genes * depth, 0),
        vmem=16,
        in_specs=in_specs,
        out_specs=[ANY, VMEM],
        out_shape=[
            jax.ShapeDtypeStruct(shape, jnp.float32),
            jax.ShapeDtypeStruct((8, 128), jnp.float32),
        ],
        scratch_shapes=[
            pltpu.VMEM((2, genes, tile), jnp.float32),
            pltpu.SemaphoreType.DMA((2,)),
        ],
        input_output_aliases=aliases,
    )(*operands)


def chunks(genes):
    units, spans, at = genes // STRIP, [], 0
    for share in SHARES[:-1]:
        size = max(1, units * share // sum(SHARES))
        spans.append((at * STRIP, size * STRIP))
        at += size
    return spans + [(at * STRIP, (units - at) * STRIP)]


def shards(counts, gene_mean, gene_std):
    groups = lax.axis_size("cell")
    outer, inner = groups, lax.axis_size("gene") // groups
    cells, genes = counts.shape
    part, counts = count_part(counts)
    terms = library_terms(part, outer * inner)
    scales = gene_scales(gene_mean[None, :], gene_std[None, :], [terms[0]])
    given = counts, scales, terms

    spans, blocks, nears, mine = chunks(genes), [], [], []
    for start, width in spans:
        (block,) = standardize(
            lambda terms, *refs, start=start: block_kernel(terms, start, *refs),
            "standardize_block",
            (cells, width),
            1,
            *given,
            [*mine, *blocks[1:]],
        )
        blocks.append(block)
        nears.append(line_near(block, outer, inner))
        if not mine:
            mine = standardize(
                rows_kernel, "standardize_rows", (genes, cells), 1, *given, [block]
            )
    lines, boths = [], []
    for q, (block, near) in enumerate(zip(blocks, nears)):
        after = boths[-1:] + (nears[q + 1 :] if q else [])
        both, arrays = line_gather(block, near, outer, inner, after)
        lines.append(arrays)
        boths.append(both)
    rows = stack(row_blocks(mine[0], groups, boths[1:2]))

    shape = (genes, genes * inner)
    scale = 1.0 / (cells * groups)
    across = [[(c, c ^ j) for c in range(groups)] for j in range(groups)]
    swap = [
        [
            (o * inner + (i + s) % inner, o * inner + i)
            for o in range(outer)
            for i in range(inner)
        ]
        for s in range(inner)
    ]
    write = functools.partial(gram_part, rows=rows, shape=shape, scale=scale)
    gram, done, sent, arrived = None, rows, [], []

    def fetch(q):
        ahead = lines[q + 1][2:3] if q + 1 < len(spans) else []
        sends = pick(lines[q], outer, inner, [done] + sent[-1:] + boths[-1:] + ahead)
        sent.append(sends[0])
        cols = [send(sends[j], "cell", across[j]) for j in range(1, groups)]
        arrived.append([sends[0]] + cols)

    fetch(0)
    for q, (start, _) in enumerate(spans):
        if q + 1 < len(spans):
            fetch(q + 1)
        own = stack([arrived[q]], [done] if q else sent[q + 1 : q + 2])
        theirs = [send(own, "gene", swap[s]) for s in range(1, inner)]
        for s, cols in enumerate([own] + theirs):
            after = sent[q + 1 : q + 2]
            if s > 0:
                after = [arrays[-1] for arrays in lines[q + 2 : q + 3]]
            gram, done = write(gram, s, start, cols, after=after)
    return gram


def solution(mesh):
    placed = (P("cell", "gene"), P("gene"), P("gene"))
    return jax.shard_map(
        shards, mesh=mesh, in_specs=placed, out_specs=P("gene", "cell"), check_vma=False
    )
```

```python
import functools

import jax
import jax.numpy as jnp
from jax import lax
from jax.experimental import pallas as pl
from jax.experimental.pallas import tpu as pltpu
from jax.sharding import PartitionSpec as P

STRIP = 128
SHARES = (2, 3, 3)
TILE = 1024
MIB = 2**20
SLACK = 8
VMEM = pl.BlockSpec(memory_space=pltpu.VMEM)
ANY = pl.BlockSpec(memory_space=pl.ANY)


def send(x, axis, pairs):
    return lax.ppermute(x, axis, pairs)


def call(kernel, name, cost, vmem=8, **kwargs):
    flops, moved, transcendentals = cost
    return pl.pallas_call(
        kernel,
        name=name,
        cost_estimate=pl.CostEstimate(
            flops=flops // SLACK,
            bytes_accessed=moved // SLACK,
            transcendentals=transcendentals // SLACK,
        ),
        compiler_params=pltpu.CompilerParams(vmem_limit_bytes=vmem * MIB),
        **kwargs,
    )


def count_kernel(counts_ref, out_ref, held_ref):
    cells, genes = counts_ref.shape
    total = jnp.zeros((cells, STRIP), jnp.float32)
    for at in range(0, genes, STRIP):
        strip = counts_ref[:, at : at + STRIP]
        held_ref[:, at : at + STRIP] = strip
        total += strip
    summed = jnp.sum(total, axis=1, keepdims=True)
    flat = jnp.broadcast_to(summed, (cells, STRIP)).T
    out_ref[...] = flat[:8, :]


def count_part(counts):
    cells, genes = counts.shape
    return call(
        count_kernel,
        "count_part",
        (cells * genes, 8 * cells * genes, 0),
        vmem=4,
        in_specs=[VMEM],
        out_specs=[VMEM] * 2,
        out_shape=[
            jax.ShapeDtypeStruct((8, cells), jnp.float32),
            jax.ShapeDtypeStruct(counts.shape, jnp.float32),
        ],
    )(counts)


def scales_kernel(mean_ref, std_ref, *refs):
    out_ref = refs[-1]
    out_ref[0:1, :] = mean_ref[...]
    out_ref[8:9, :] = 1.0 / jnp.maximum(std_ref[...], 0.1)


def gene_scales(mean, std, after):
    genes = mean.shape[1]
    return call(
        scales_kernel,
        "gene_scales",
        (2 * genes, 72 * genes, 0),
        vmem=1,
        in_specs=[VMEM] * 2 + [ANY] * len(after),
        out_specs=VMEM,
        out_shape=jax.ShapeDtypeStruct((16, genes), jnp.float32),
    )(mean, std, *after)


def add_kernel(a_ref, b_ref, out_ref):
    out_ref[...] = a_ref[...] + b_ref[...]


def add(a, b):
    return call(
        add_kernel,
        "add_terms",
        (a.size, 12 * a.size, 0),
        vmem=1,
        in_specs=[VMEM] * 2,
        out_specs=VMEM,
        out_shape=jax.ShapeDtypeStruct(a.shape, a.dtype),
    )(a, b)


def library_terms(part, size):
    terms, step = [part], 1
    while step < size:
        part = terms[0] if len(terms) == 1 else add(*terms)
        terms = [part, send(part, "gene", [(g, g ^ step) for g in range(size)])]
        step *= 2
    return terms


def scaled_strip(counts_ref, genes_ref, factor, at):
    normal = jnp.log1p(counts_ref[:, at] * factor)
    return jnp.minimum((normal - genes_ref[0:1, at]) * genes_ref[8:9, at], 10.0)


def cell_factor(sums, cells):
    library = sums[0][:1, :]
    for ref in sums[1:]:
        library = library + ref[:1, :]
    return jnp.broadcast_to(10000.0 / library, (STRIP, cells)).T


def block_kernel(terms, start, counts_ref, genes_ref, *refs):
    factor = cell_factor(refs[:terms], counts_ref.shape[0])
    out_ref = refs[-1]

    @pl.loop(0, out_ref.shape[1] // STRIP)
    def _(k):
        there = pl.multiple_of(k * STRIP, STRIP)
        at = pl.ds(start + there, STRIP)
        scaled = scaled_strip(counts_ref, genes_ref, factor, at)
        out_ref[:, pl.ds(there, STRIP)] = scaled.astype(jnp.bfloat16)


def rows_kernel(terms, counts_ref, genes_ref, *refs):
    factor = cell_factor(refs[:terms], counts_ref.shape[0])
    out_ref = refs[-1]

    @pl.loop(0, counts_ref.shape[1] // STRIP)
    def _(k):
        at = pl.ds(pl.multiple_of(k * STRIP, STRIP), STRIP)
        scaled = scaled_strip(counts_ref, genes_ref, factor, at)
        out_ref[at, :] = scaled.T.astype(jnp.bfloat16)


def standardize(kernel, name, shape, pieces, counts, scales, terms, after=()):
    size = pieces * shape[0] * shape[1]
    return call(
        functools.partial(kernel, len(terms)),
        name,
        (20 * size, 6 * size, size),
        in_specs=[VMEM] * (2 + len(terms)) + [ANY] * len(after),
        out_specs=[VMEM] * pieces,
        out_shape=[jax.ShapeDtypeStruct(shape, jnp.bfloat16)] * pieces,
    )(counts, scales, *terms, *after)


def split_kernel(one_ref, two_ref, *refs):
    top_ref, low_ref = refs[-2:]
    half = top_ref.shape[0]
    top_ref[...] = one_ref[:half, :]
    low_ref[...] = two_ref[half:, :]


def row_blocks(mine, groups, after):
    def cross(x, j):
        return send(x, "cell", [(c, c ^ j) for c in range(groups)])

    if groups != 4:
        return [[mine]] + [[cross(mine, j)] for j in range(1, groups)], []
    one, two = cross(mine, 1), cross(mine, 2)
    half = jax.ShapeDtypeStruct((mine.shape[0] // 2, mine.shape[1]), mine.dtype)
    top, low = call(
        split_kernel,
        "split_rows",
        (0, 4 * mine.size, 0),
        vmem=4,
        in_specs=[VMEM] * 2 + [ANY] * len(after),
        out_specs=[VMEM] * 2,
        out_shape=[half] * 2,
    )(one, two, *after)
    return [[mine], [one], [two], [cross(top, 2), cross(low, 1)]], [top]


def stack_kernel(places, *refs):
    out_ref = refs[-1]
    for ref, (line, at) in zip(refs, places):
        high, wide = ref.shape
        out_ref[line : line + high, at : at + wide] = ref[...]


def stack(columns, after=()):
    places, blocks, at = [], [], 0
    for column in columns:
        line = 0
        for x in column:
            places.append((line, at))
            blocks.append(x)
            line += x.shape[0]
        at += column[0].shape[1]
    return call(
        functools.partial(stack_kernel, places),
        "stack_blocks",
        (0, 4 * line * at, 0),
        vmem=4,
        in_specs=[VMEM] * len(blocks) + [ANY] * len(after),
        out_specs=VMEM,
        out_shape=jax.ShapeDtypeStruct((line, at), blocks[0].dtype),
    )(*blocks, *after)


def line_pairs(outer, inner, moves):
    return [(a * inner + i, b * inner + i) for a, b in moves for i in range(inner)]


def line_move(x, outer, inner, moves):
    return send(x, "gene", line_pairs(outer, inner, moves))


def line_near(block, outer, inner):
    if outer == 4:
        return line_move(block, outer, inner, [(0, 1), (1, 0), (2, 3), (3, 2)])
    return line_move(block, outer, inner, [(o, o + 1) for o in range(outer - 1)])


def line_gather(block, near, outer, inner, after):
    def move(x, moves):
        return line_move(x, outer, inner, moves)

    if outer == 4:
        both = stack([[block, near]], after)
        across = move(both, [(1, 2), (2, 1)])
        ends = move(across, [(1, 0), (2, 3)])
        return both, [block, near, across, ends]
    ups, downs = [block, near], [block]
    for h in range(1, outer):
        if h > 1:
            ups.append(move(ups[-1], [(o, o + 1) for o in range(h - 1, outer - 1)]))
        downs.append(move(downs[-1], [(o, o - 1) for o in range(1, outer - h + 1)]))
    return block, [block] + ups[1:] + downs[1:]


def line_place(outer, at, wanted):
    if outer == 4:
        far = {0: (2, 3), 1: (2, 3), 2: (1, 0), 3: (1, 0)}[at]
        if wanted in far:
            return far.index(wanted) + (2 if at in (1, 2) else 4)
        return int(wanted != at)
    if wanted <= at:
        return at - wanted
    return outer - 1 + wanted - at


def pick_kernel(groups, outer, inner, arrays, *refs):
    outs = refs[-groups:]
    depth = outs[0].shape[0]
    sources = [
        (ref, part * depth)
        for ref in refs[:arrays]
        for part in range(ref.shape[0] // depth)
    ]
    cell_at = lax.axis_index("cell")
    line_at = lax.div(lax.axis_index("gene"), jnp.int32(inner))
    pairs = [(o, to) for o in range(outer) for to in range(outer)]
    for j in range(groups):
        here = line_at * outer + lax.bitwise_xor(cell_at, jnp.int32(j))
        for k, (ref, line) in enumerate(sources):
            found = [o * outer + to for o, to in pairs if line_place(outer, o, to) == k]
            match = functools.reduce(jnp.logical_or, [here == x for x in found])

            @pl.when(match)
            def _():
                outs[j][...] = ref[line : line + depth, :]


def pick(arrays, outer, inner, after):
    depth, width = arrays[0].shape
    return call(
        functools.partial(pick_kernel, outer, outer, inner, len(arrays)),
        "pick_blocks",
        (0, 4 * outer * depth * width, 0),
        vmem=4,
        in_specs=[VMEM] * len(arrays) + [ANY] * len(after),
        out_specs=[VMEM] * outer,
        out_shape=[jax.ShapeDtypeStruct((depth, width), arrays[0].dtype)] * outer,
    )(*arrays, *after)


def gram_kernel(inner, step, start, scale, rows_ref, cols_ref, *refs):
    out_ref, done_ref, tiles, sems = refs[-4:]
    tile, width = tiles.shape[1:]
    genes = rows_ref.shape[0]
    owner = lax.rem(lax.axis_index("gene") + step, jnp.int32(inner))
    at = pl.multiple_of(owner * genes + start, STRIP)

    def give(m):
        return pltpu.make_async_copy(
            tiles.at[m % 2],
            out_ref.at[pl.ds(m * tile, tile), pl.ds(at, width)],
            sems.at[m % 2],
        )

    count = genes // tile
    for m in range(count):
        if m >= 2:
            give(m - 2).wait()
        total = jnp.dot(
            rows_ref[m * tile : (m + 1) * tile, :],
            cols_ref[...],
            preferred_element_type=jnp.float32,
        )
        tiles[m % 2] = total * scale
        give(m).start()
    for m in range(max(count - 2, 0), count):
        give(m).wait()
    done_ref[...] = jnp.zeros_like(done_ref)


def gram_part(gram, step, start, cols, rows, shape, scale, after=()):
    genes, depth = rows.shape
    width = cols.shape[1]
    tile = min(TILE, genes)
    inner = shape[1] // genes
    operands = [rows, cols, *after]
    in_specs = [VMEM, VMEM] + [ANY] * len(after)
    aliases = {}
    if gram is not None:
        aliases = {len(operands): 0}
        in_specs.append(ANY)
        operands.append(gram)
    return call(
        functools.partial(gram_kernel, inner, step, start, scale),
        "gram_part",
        (2 * genes * depth * width, 4 * genes * width + 2 * genes * depth, 0),
        vmem=24,
        in_specs=in_specs,
        out_specs=[ANY, VMEM],
        out_shape=[
            jax.ShapeDtypeStruct(shape, jnp.float32),
            jax.ShapeDtypeStruct((8, 128), jnp.float32),
        ],
        scratch_shapes=[
            pltpu.VMEM((2, tile, width), jnp.float32),
            pltpu.SemaphoreType.DMA((2,)),
        ],
        input_output_aliases=aliases,
    )(*operands)


def chunks(genes):
    units, spans, at = genes // STRIP, [], 0
    for share in SHARES[:-1]:
        size = max(1, units * share // sum(SHARES))
        spans.append((at * STRIP, size * STRIP))
        at += size
    return spans + [(at * STRIP, (units - at) * STRIP)]


def shards(counts, gene_mean, gene_std):
    groups = lax.axis_size("cell")
    outer, inner = groups, lax.axis_size("gene") // groups
    cells, genes = counts.shape
    part, counts = count_part(counts)
    terms = library_terms(part, outer * inner)
    scales = gene_scales(gene_mean[None, :], gene_std[None, :], [terms[0]])
    given = counts, scales, terms

    lines, boths, nears, blocks, after = [], [], [], [], []
    spans = chunks(genes)

    def standard(q, after):
        start, width = spans[q]
        (block,) = standardize(
            lambda terms, *refs: block_kernel(terms, start, *refs),
            "standardize_block",
            (cells, width),
            1,
            *given,
            after,
        )
        blocks.append(block)
        nears.append(line_near(block, outer, inner))

    def gather(q, after):
        both, arrays = line_gather(blocks[q], nears[q], outer, inner, after)
        lines.append(arrays)
        boths.append(both)

    standard(0, [])
    (mine,) = standardize(
        rows_kernel, "standardize_rows", (genes, cells), 1, *given, blocks[:1]
    )
    standard(1, [mine])
    gather(0, [blocks[1]])
    standard(2, [boths[0]])
    columns, parts = row_blocks(mine, groups, [boths[0]])
    gather(1, [boths[0], lines[0][2], *parts])
    gather(2, [boths[1], lines[1][2]])
    rows = stack(columns)

    shape = (genes, genes * inner)
    scale = 1.0 / (cells * groups)
    across = [[(c, c ^ j) for c in range(groups)] for j in range(groups)]
    swap = [
        [
            (o * inner + (i + s) % inner, o * inner + i)
            for o in range(outer)
            for i in range(inner)
        ]
        for s in range(inner)
    ]
    write = functools.partial(gram_part, rows=rows, shape=shape, scale=scale)
    gram, done, sent, arrived = None, rows, [], []

    def fetch(q):
        ahead = lines[q + 1][2:3] if q + 1 < len(spans) else []
        sends = pick(lines[q], outer, inner, [done] + sent[-1:] + boths[-1:] + ahead)
        sent.append(sends[0])
        cols = [send(sends[j], "cell", across[j]) for j in range(1, groups)]
        arrived.append([sends[0]] + cols)

    fetch(0)
    for q, (start, _) in enumerate(spans):
        if q + 1 < len(spans):
            fetch(q + 1)
        own = stack([arrived[q]], [done] if q else sent[q + 1 : q + 2])
        theirs = [send(own, "gene", swap[s]) for s in range(1, inner)]
        for s, cols in enumerate([own] + theirs):
            after = sent[q + 1 : q + 2]
            if s > 0:
                after = [arrays[-1] for arrays in lines[q + 2 : q + 3]]
            gram, done = write(gram, s, start, cols, after=after)
    return gram


def solution(mesh):
    placed = (P("cell", "gene"), P("gene"), P("gene"))
    return jax.shard_map(
        shards, mesh=mesh, in_specs=placed, out_specs=P("gene", "cell"), check_vma=False
    )
```

```python
import functools

import jax
import jax.numpy as jnp
from jax import lax
from jax.experimental import pallas as pl
from jax.experimental.pallas import tpu as pltpu
from jax.sharding import PartitionSpec as P

STRIP = 128
SHARES = (3, 3, 2)
TILE = 1024
MIB = 2**20
SLACK = 8
VMEM = pl.BlockSpec(memory_space=pltpu.VMEM)
ANY = pl.BlockSpec(memory_space=pl.ANY)


def send(x, axis, pairs):
    return lax.ppermute(x, axis, pairs)


def call(kernel, name, cost, vmem=8, **kwargs):
    flops, moved, transcendentals = cost
    return pl.pallas_call(
        kernel,
        name=name,
        cost_estimate=pl.CostEstimate(
            flops=flops // SLACK,
            bytes_accessed=moved // SLACK,
            transcendentals=transcendentals // SLACK,
        ),
        compiler_params=pltpu.CompilerParams(vmem_limit_bytes=vmem * MIB),
        **kwargs,
    )


def count_kernel(counts_ref, out_ref, held_ref):
    cells, genes = counts_ref.shape
    total = jnp.zeros((cells, STRIP), jnp.float32)
    for at in range(0, genes, STRIP):
        strip = counts_ref[:, at : at + STRIP]
        held_ref[:, at : at + STRIP] = strip
        total += strip
    summed = jnp.sum(total, axis=1, keepdims=True)
    flat = jnp.broadcast_to(summed, (cells, STRIP)).T
    out_ref[...] = flat[:8, :]


def count_part(counts):
    cells, genes = counts.shape
    return call(
        count_kernel,
        "count_part",
        (cells * genes, 8 * cells * genes, 0),
        vmem=4,
        in_specs=[VMEM],
        out_specs=[VMEM] * 2,
        out_shape=[
            jax.ShapeDtypeStruct((8, cells), jnp.float32),
            jax.ShapeDtypeStruct(counts.shape, jnp.float32),
        ],
    )(counts)


def scales_kernel(mean_ref, std_ref, *refs):
    out_ref = refs[-1]
    out_ref[0:1, :] = mean_ref[...]
    out_ref[8:9, :] = 1.0 / jnp.maximum(std_ref[...], 0.1)


def gene_scales(mean, std, after):
    genes = mean.shape[1]
    return call(
        scales_kernel,
        "gene_scales",
        (2 * genes, 72 * genes, 0),
        vmem=1,
        in_specs=[VMEM] * 2 + [ANY] * len(after),
        out_specs=VMEM,
        out_shape=jax.ShapeDtypeStruct((16, genes), jnp.float32),
    )(mean, std, *after)


def add_kernel(a_ref, b_ref, out_ref):
    out_ref[...] = a_ref[...] + b_ref[...]


def add(a, b):
    return call(
        add_kernel,
        "add_terms",
        (a.size, 12 * a.size, 0),
        vmem=1,
        in_specs=[VMEM] * 2,
        out_specs=VMEM,
        out_shape=jax.ShapeDtypeStruct(a.shape, a.dtype),
    )(a, b)


def library_terms(part, size):
    terms, step = [part], 1
    while step < size:
        part = terms[0] if len(terms) == 1 else add(*terms)
        terms = [part, send(part, "gene", [(g, g ^ step) for g in range(size)])]
        step *= 2
    return terms


def scaled_strip(counts_ref, genes_ref, factor, at):
    normal = jnp.log1p(counts_ref[:, at] * factor)
    return jnp.minimum((normal - genes_ref[0:1, at]) * genes_ref[8:9, at], 10.0)


def cell_factor(sums, cells):
    library = sums[0][:1, :]
    for ref in sums[1:]:
        library = library + ref[:1, :]
    return jnp.broadcast_to(10000.0 / library, (STRIP, cells)).T


def block_kernel(terms, start, counts_ref, genes_ref, *refs):
    factor = cell_factor(refs[:terms], counts_ref.shape[0])
    out_ref = refs[-1]

    @pl.loop(0, out_ref.shape[1] // STRIP)
    def _(k):
        there = pl.multiple_of(k * STRIP, STRIP)
        at = pl.ds(start + there, STRIP)
        scaled = scaled_strip(counts_ref, genes_ref, factor, at)
        out_ref[:, pl.ds(there, STRIP)] = scaled.astype(jnp.bfloat16)


def rows_kernel(terms, counts_ref, genes_ref, *refs):
    factor = cell_factor(refs[:terms], counts_ref.shape[0])
    out_ref = refs[-1]

    @pl.loop(0, counts_ref.shape[1] // STRIP)
    def _(k):
        at = pl.ds(pl.multiple_of(k * STRIP, STRIP), STRIP)
        scaled = scaled_strip(counts_ref, genes_ref, factor, at)
        out_ref[at, :] = scaled.T.astype(jnp.bfloat16)


def standardize(kernel, name, shape, pieces, counts, scales, terms, after=()):
    size = pieces * shape[0] * shape[1]
    return call(
        functools.partial(kernel, len(terms)),
        name,
        (20 * size, 6 * size, size),
        in_specs=[VMEM] * (2 + len(terms)) + [ANY] * len(after),
        out_specs=[VMEM] * pieces,
        out_shape=[jax.ShapeDtypeStruct(shape, jnp.bfloat16)] * pieces,
    )(counts, scales, *terms, *after)


def split_kernel(one_ref, two_ref, *refs):
    top_ref, low_ref = refs[-2:]
    half = top_ref.shape[0]
    top_ref[...] = one_ref[:half, :]
    low_ref[...] = two_ref[half:, :]


def row_blocks(mine, groups, after):
    def cross(x, j):
        return send(x, "cell", [(c, c ^ j) for c in range(groups)])

    if groups != 4:
        return [[mine]] + [[cross(mine, j)] for j in range(1, groups)]
    one, two = cross(mine, 1), cross(mine, 2)
    half = jax.ShapeDtypeStruct((mine.shape[0] // 2, mine.shape[1]), mine.dtype)
    top, low = call(
        split_kernel,
        "split_rows",
        (0, 4 * mine.size, 0),
        vmem=4,
        in_specs=[VMEM] * 2 + [ANY] * len(after),
        out_specs=[VMEM] * 2,
        out_shape=[half] * 2,
    )(one, two, *after)
    return [[mine], [one], [two], [cross(top, 2), cross(low, 1)]]


def stack_kernel(places, *refs):
    out_ref = refs[-1]
    for ref, (line, at) in zip(refs, places):
        high, wide = ref.shape
        out_ref[line : line + high, at : at + wide] = ref[...]


def stack(columns, after=()):
    places, blocks, at = [], [], 0
    for column in columns:
        line = 0
        for x in column:
            places.append((line, at))
            blocks.append(x)
            line += x.shape[0]
        at += column[0].shape[1]
    return call(
        functools.partial(stack_kernel, places),
        "stack_blocks",
        (0, 4 * line * at, 0),
        vmem=4,
        in_specs=[VMEM] * len(blocks) + [ANY] * len(after),
        out_specs=VMEM,
        out_shape=jax.ShapeDtypeStruct((line, at), blocks[0].dtype),
    )(*blocks, *after)


def line_pairs(outer, inner, moves):
    return [(a * inner + i, b * inner + i) for a, b in moves for i in range(inner)]


def line_move(x, outer, inner, moves):
    return send(x, "gene", line_pairs(outer, inner, moves))


def line_near(block, outer, inner):
    if outer == 4:
        return line_move(block, outer, inner, [(0, 1), (1, 0), (2, 3), (3, 2)])
    return line_move(block, outer, inner, [(o, o + 1) for o in range(outer - 1)])


def line_gather(block, near, outer, inner, after):
    def move(x, moves):
        return line_move(x, outer, inner, moves)

    if outer == 4:
        both = stack([[block, near]], after)
        across = move(both, [(1, 2), (2, 1)])
        ends = move(across, [(1, 0), (2, 3)])
        return both, [block, near, across, ends]
    ups, downs = [block, near], [block]
    for h in range(1, outer):
        if h > 1:
            ups.append(move(ups[-1], [(o, o + 1) for o in range(h - 1, outer - 1)]))
        downs.append(move(downs[-1], [(o, o - 1) for o in range(1, outer - h + 1)]))
    return block, [block] + ups[1:] + downs[1:]


def line_place(outer, at, wanted):
    if outer == 4:
        far = {0: (2, 3), 1: (2, 3), 2: (1, 0), 3: (1, 0)}[at]
        if wanted in far:
            return far.index(wanted) + (2 if at in (1, 2) else 4)
        return int(wanted != at)
    if wanted <= at:
        return at - wanted
    return outer - 1 + wanted - at


def pick_kernel(groups, outer, inner, arrays, *refs):
    outs = refs[-groups:]
    depth = outs[0].shape[0]
    sources = [
        (ref, part * depth)
        for ref in refs[:arrays]
        for part in range(ref.shape[0] // depth)
    ]
    cell_at = lax.axis_index("cell")
    line_at = lax.div(lax.axis_index("gene"), jnp.int32(inner))
    pairs = [(o, to) for o in range(outer) for to in range(outer)]
    for j in range(groups):
        here = line_at * outer + lax.bitwise_xor(cell_at, jnp.int32(j))
        for k, (ref, line) in enumerate(sources):
            found = [o * outer + to for o, to in pairs if line_place(outer, o, to) == k]
            match = functools.reduce(jnp.logical_or, [here == x for x in found])

            @pl.when(match)
            def _():
                outs[j][...] = ref[line : line + depth, :]


def pick(arrays, outer, inner, after):
    depth, width = arrays[0].shape
    return call(
        functools.partial(pick_kernel, outer, outer, inner, len(arrays)),
        "pick_blocks",
        (0, 4 * outer * depth * width, 0),
        vmem=4,
        in_specs=[VMEM] * len(arrays) + [ANY] * len(after),
        out_specs=[VMEM] * outer,
        out_shape=[jax.ShapeDtypeStruct((depth, width), arrays[0].dtype)] * outer,
    )(*arrays, *after)


def gram_kernel(inner, steps, start, scale, rows_ref, *refs):
    cols = refs[: len(steps)]
    out_ref, done_ref, tiles, sems = refs[-4:]
    tile, width = tiles.shape[1:]
    genes = rows_ref.shape[0]

    def give(n):
        m, k = divmod(n, len(steps))
        owner = lax.rem(lax.axis_index("gene") + steps[k], jnp.int32(inner))
        at = pl.multiple_of(owner * genes + start, STRIP)
        return pltpu.make_async_copy(
            tiles.at[n % 2],
            out_ref.at[pl.ds(m * tile, tile), pl.ds(at, width)],
            sems.at[n % 2],
        )

    count = genes // tile * len(steps)
    for n in range(count):
        m, k = divmod(n, len(steps))
        if n >= 2:
            give(n - 2).wait()
        total = jnp.dot(
            rows_ref[m * tile : (m + 1) * tile, :],
            cols[k][...],
            preferred_element_type=jnp.float32,
        )
        tiles[n % 2] = total * scale
        give(n).start()
    for n in range(max(count - 2, 0), count):
        give(n).wait()
    done_ref[...] = jnp.zeros_like(done_ref)


def gram_part(gram, steps, start, cols, rows, shape, scale, after=()):
    genes, depth = rows.shape
    width = cols[0].shape[1]
    tile = min(TILE, genes)
    inner = shape[1] // genes
    operands = [rows, *cols, *after]
    in_specs = [VMEM] * (1 + len(cols)) + [ANY] * len(after)
    aliases = {}
    if gram is not None:
        aliases = {len(operands): 0}
        in_specs.append(ANY)
        operands.append(gram)
    return call(
        functools.partial(gram_kernel, inner, steps, start, scale),
        "gram_part",
        (
            2 * len(cols) * genes * depth * width,
            4 * len(cols) * genes * width + 2 * genes * depth,
            0,
        ),
        vmem=24,
        in_specs=in_specs,
        out_specs=[ANY, VMEM],
        out_shape=[
            jax.ShapeDtypeStruct(shape, jnp.float32),
            jax.ShapeDtypeStruct((8, 128), jnp.float32),
        ],
        scratch_shapes=[
            pltpu.VMEM((2, tile, width), jnp.float32),
            pltpu.SemaphoreType.DMA((2,)),
        ],
        input_output_aliases=aliases,
    )(*operands)


def chunks(genes):
    units, spans, at = genes // STRIP, [], 0
    for share in SHARES[:-1]:
        size = max(1, units * share // sum(SHARES))
        spans.append((at * STRIP, size * STRIP))
        at += size
    return spans + [(at * STRIP, (units - at) * STRIP)]


def shards(counts, gene_mean, gene_std):
    groups = lax.axis_size("cell")
    outer, inner = groups, lax.axis_size("gene") // groups
    cells, genes = counts.shape
    part, counts = count_part(counts)
    terms = library_terms(part, outer * inner)
    scales = gene_scales(gene_mean[None, :], gene_std[None, :], [terms[0]])
    given = counts, scales, terms

    spans, blocks, nears, mine = chunks(genes), [], [], []
    for start, width in spans:
        (block,) = standardize(
            lambda terms, *refs, start=start: block_kernel(terms, start, *refs),
            "standardize_block",
            (cells, width),
            1,
            *given,
            [*mine, *blocks[1:]],
        )
        blocks.append(block)
        nears.append(line_near(block, outer, inner))
        if not mine:
            mine = standardize(
                rows_kernel, "standardize_rows", (genes, cells), 1, *given, [block]
            )
    lines, boths = [], []
    for q, (block, near) in enumerate(zip(blocks, nears)):
        after = boths[-1:] + (nears[q + 1 :] if q else [])
        both, arrays = line_gather(block, near, outer, inner, after)
        lines.append(arrays)
        boths.append(both)
    rows = stack(row_blocks(mine[0], groups, boths[1:2]))

    shape = (genes, genes * inner)
    scale = 1.0 / (cells * groups)
    across = [[(c, c ^ j) for c in range(groups)] for j in range(groups)]
    swap = [
        [
            (o * inner + (i + s) % inner, o * inner + i)
            for o in range(outer)
            for i in range(inner)
        ]
        for s in range(inner)
    ]
    write = functools.partial(gram_part, rows=rows, shape=shape, scale=scale)
    gram, done, sent, arrived = None, rows, [], []

    def fetch(q):
        ahead = lines[q + 1][2:3] if q + 1 < len(spans) else []
        sends = pick(lines[q], outer, inner, [done] + sent[-1:] + boths[-1:] + ahead)
        sent.append(sends[0])
        cols = [send(sends[j], "cell", across[j]) for j in range(1, groups)]
        arrived.append([sends[0]] + cols)

    fetch(0)
    for q, (start, _) in enumerate(spans):
        if q + 1 < len(spans):
            fetch(q + 1)
        own = stack([arrived[q]], [done] * (q > 0) + sent[q + 1 : q + 2])
        theirs = [send(own, "gene", swap[s]) for s in range(1, inner)]
        parts = list(enumerate([own] + theirs))
        for part in [parts] if q + 1 < len(spans) else [[x] for x in parts]:
            steps, cols = zip(*part)
            gram, done = write(gram, steps, start, cols, after=sent[q + 1 : q + 2])
    return gram


def solution(mesh):
    placed = (P("cell", "gene"), P("gene"), P("gene"))
    return jax.shard_map(
        shards, mesh=mesh, in_specs=placed, out_specs=P("gene", "cell"), check_vma=False
    )
```

```python
import functools

import jax
import jax.numpy as jnp
from jax import lax
from jax.experimental import pallas as pl
from jax.experimental.pallas import tpu as pltpu
from jax.sharding import PartitionSpec as P

STRIP = 128
SHARES = (2, 2, 2, 2)
TILE = 1024
MIB = 2**20
SLACK = 8
VMEM = pl.BlockSpec(memory_space=pltpu.VMEM)
ANY = pl.BlockSpec(memory_space=pl.ANY)


def send(x, axis, pairs):
    return lax.ppermute(x, axis, pairs)


def call(kernel, name, cost, vmem=8, **kwargs):
    flops, moved, transcendentals = cost
    return pl.pallas_call(
        kernel,
        name=name,
        cost_estimate=pl.CostEstimate(
            flops=flops // SLACK,
            bytes_accessed=moved // SLACK,
            transcendentals=transcendentals // SLACK,
        ),
        compiler_params=pltpu.CompilerParams(vmem_limit_bytes=vmem * MIB),
        **kwargs,
    )


def count_kernel(counts_ref, out_ref, held_ref):
    cells, genes = counts_ref.shape
    total = jnp.zeros((cells, STRIP), jnp.float32)
    for at in range(0, genes, STRIP):
        strip = counts_ref[:, at : at + STRIP]
        held_ref[:, at : at + STRIP] = strip
        total += strip
    summed = jnp.sum(total, axis=1, keepdims=True)
    flat = jnp.broadcast_to(summed, (cells, STRIP)).T
    out_ref[...] = flat[:8, :]


def count_part(counts):
    cells, genes = counts.shape
    return call(
        count_kernel,
        "count_part",
        (cells * genes, 8 * cells * genes, 0),
        vmem=4,
        in_specs=[VMEM],
        out_specs=[VMEM] * 2,
        out_shape=[
            jax.ShapeDtypeStruct((8, cells), jnp.float32),
            jax.ShapeDtypeStruct(counts.shape, jnp.float32),
        ],
    )(counts)


def scales_kernel(mean_ref, std_ref, *refs):
    out_ref = refs[-1]
    out_ref[0:1, :] = mean_ref[...]
    out_ref[8:9, :] = 1.0 / jnp.maximum(std_ref[...], 0.1)


def gene_scales(mean, std, after):
    genes = mean.shape[1]
    return call(
        scales_kernel,
        "gene_scales",
        (2 * genes, 72 * genes, 0),
        vmem=1,
        in_specs=[VMEM] * 2 + [ANY] * len(after),
        out_specs=VMEM,
        out_shape=jax.ShapeDtypeStruct((16, genes), jnp.float32),
    )(mean, std, *after)


def add_kernel(a_ref, b_ref, out_ref):
    out_ref[...] = a_ref[...] + b_ref[...]


def add(a, b):
    return call(
        add_kernel,
        "add_terms",
        (a.size, 12 * a.size, 0),
        vmem=1,
        in_specs=[VMEM] * 2,
        out_specs=VMEM,
        out_shape=jax.ShapeDtypeStruct(a.shape, a.dtype),
    )(a, b)


def library_terms(part, size):
    terms, step = [part], 1
    while step < size:
        part = terms[0] if len(terms) == 1 else add(*terms)
        terms = [part, send(part, "gene", [(g, g ^ step) for g in range(size)])]
        step *= 2
    return terms


def scaled_strip(counts_ref, genes_ref, factor, at):
    normal = jnp.log1p(counts_ref[:, at] * factor)
    return jnp.minimum((normal - genes_ref[0:1, at]) * genes_ref[8:9, at], 10.0)


def cell_factor(sums, cells):
    library = sums[0][:1, :]
    for ref in sums[1:]:
        library = library + ref[:1, :]
    return jnp.broadcast_to(10000.0 / library, (STRIP, cells)).T


def block_kernel(terms, start, counts_ref, genes_ref, *refs):
    factor = cell_factor(refs[:terms], counts_ref.shape[0])
    out_ref = refs[-1]

    @pl.loop(0, out_ref.shape[1] // STRIP)
    def _(k):
        there = pl.multiple_of(k * STRIP, STRIP)
        at = pl.ds(start + there, STRIP)
        scaled = scaled_strip(counts_ref, genes_ref, factor, at)
        out_ref[:, pl.ds(there, STRIP)] = scaled.astype(jnp.bfloat16)


def rows_kernel(terms, counts_ref, genes_ref, *refs):
    factor = cell_factor(refs[:terms], counts_ref.shape[0])
    out_ref = refs[-1]

    @pl.loop(0, counts_ref.shape[1] // STRIP)
    def _(k):
        at = pl.ds(pl.multiple_of(k * STRIP, STRIP), STRIP)
        scaled = scaled_strip(counts_ref, genes_ref, factor, at)
        out_ref[at, :] = scaled.T.astype(jnp.bfloat16)


def standardize(kernel, name, shape, pieces, counts, scales, terms, after=()):
    size = pieces * shape[0] * shape[1]
    return call(
        functools.partial(kernel, len(terms)),
        name,
        (20 * size, 6 * size, size),
        in_specs=[VMEM] * (2 + len(terms)) + [ANY] * len(after),
        out_specs=[VMEM] * pieces,
        out_shape=[jax.ShapeDtypeStruct(shape, jnp.bfloat16)] * pieces,
    )(counts, scales, *terms, *after)


def split_kernel(one_ref, two_ref, *refs):
    top_ref, low_ref = refs[-2:]
    half = top_ref.shape[0]
    top_ref[...] = one_ref[:half, :]
    low_ref[...] = two_ref[half:, :]


def row_blocks(mine, groups, after):
    def cross(x, j):
        return send(x, "cell", [(c, c ^ j) for c in range(groups)])

    if groups != 4:
        return [[mine]] + [[cross(mine, j)] for j in range(1, groups)]
    one, two = cross(mine, 1), cross(mine, 2)
    half = jax.ShapeDtypeStruct((mine.shape[0] // 2, mine.shape[1]), mine.dtype)
    top, low = call(
        split_kernel,
        "split_rows",
        (0, 4 * mine.size, 0),
        vmem=4,
        in_specs=[VMEM] * 2 + [ANY] * len(after),
        out_specs=[VMEM] * 2,
        out_shape=[half] * 2,
    )(one, two, *after)
    return [[mine], [one], [two], [cross(top, 2), cross(low, 1)]]


def stack_kernel(places, *refs):
    out_ref = refs[-1]
    for ref, (line, at) in zip(refs, places):
        high, wide = ref.shape
        out_ref[line : line + high, at : at + wide] = ref[...]


def stack(columns, after=()):
    places, blocks, at = [], [], 0
    for column in columns:
        line = 0
        for x in column:
            places.append((line, at))
            blocks.append(x)
            line += x.shape[0]
        at += column[0].shape[1]
    return call(
        functools.partial(stack_kernel, places),
        "stack_blocks",
        (0, 4 * line * at, 0),
        vmem=4,
        in_specs=[VMEM] * len(blocks) + [ANY] * len(after),
        out_specs=VMEM,
        out_shape=jax.ShapeDtypeStruct((line, at), blocks[0].dtype),
    )(*blocks, *after)


def line_pairs(outer, inner, moves):
    return [(a * inner + i, b * inner + i) for a, b in moves for i in range(inner)]


def line_move(x, outer, inner, moves):
    return send(x, "gene", line_pairs(outer, inner, moves))


def line_near(block, outer, inner):
    if outer == 4:
        return line_move(block, outer, inner, [(0, 1), (1, 0), (2, 3), (3, 2)])
    return line_move(block, outer, inner, [(o, o + 1) for o in range(outer - 1)])


def line_gather(block, near, outer, inner, after):
    def move(x, moves):
        return line_move(x, outer, inner, moves)

    if outer == 4:
        both = stack([[block, near]], after)
        across = move(both, [(1, 2), (2, 1)])
        ends = move(across, [(1, 0), (2, 3)])
        return both, [block, near, across, ends]
    ups, downs = [block, near], [block]
    for h in range(1, outer):
        if h > 1:
            ups.append(move(ups[-1], [(o, o + 1) for o in range(h - 1, outer - 1)]))
        downs.append(move(downs[-1], [(o, o - 1) for o in range(1, outer - h + 1)]))
    return block, [block] + ups[1:] + downs[1:]


def line_place(outer, at, wanted):
    if outer == 4:
        far = {0: (2, 3), 1: (2, 3), 2: (1, 0), 3: (1, 0)}[at]
        if wanted in far:
            return far.index(wanted) + (2 if at in (1, 2) else 4)
        return int(wanted != at)
    if wanted <= at:
        return at - wanted
    return outer - 1 + wanted - at


def pick_kernel(groups, outer, inner, arrays, *refs):
    outs = refs[-groups:]
    depth = outs[0].shape[0]
    sources = [
        (ref, part * depth)
        for ref in refs[:arrays]
        for part in range(ref.shape[0] // depth)
    ]
    cell_at = lax.axis_index("cell")
    line_at = lax.div(lax.axis_index("gene"), jnp.int32(inner))
    pairs = [(o, to) for o in range(outer) for to in range(outer)]
    for j in range(groups):
        here = line_at * outer + lax.bitwise_xor(cell_at, jnp.int32(j))
        for k, (ref, line) in enumerate(sources):
            found = [o * outer + to for o, to in pairs if line_place(outer, o, to) == k]
            match = functools.reduce(jnp.logical_or, [here == x for x in found])

            @pl.when(match)
            def _():
                outs[j][...] = ref[line : line + depth, :]


def pick(arrays, outer, inner, after):
    depth, width = arrays[0].shape
    return call(
        functools.partial(pick_kernel, outer, outer, inner, len(arrays)),
        "pick_blocks",
        (0, 4 * outer * depth * width, 0),
        vmem=4,
        in_specs=[VMEM] * len(arrays) + [ANY] * len(after),
        out_specs=[VMEM] * outer,
        out_shape=[jax.ShapeDtypeStruct((depth, width), arrays[0].dtype)] * outer,
    )(*arrays, *after)


def gram_kernel(inner, steps, start, scale, rows_ref, *refs):
    cols = refs[: len(steps)]
    out_ref, done_ref, tiles, sems = refs[-4:]
    tile, width = tiles.shape[1:]
    genes = rows_ref.shape[0]

    def give(n):
        m, k = divmod(n, len(steps))
        owner = lax.rem(lax.axis_index("gene") + steps[k], jnp.int32(inner))
        at = pl.multiple_of(owner * genes + start, STRIP)
        return pltpu.make_async_copy(
            tiles.at[n % 2],
            out_ref.at[pl.ds(m * tile, tile), pl.ds(at, width)],
            sems.at[n % 2],
        )

    count = genes // tile * len(steps)
    for n in range(count):
        m, k = divmod(n, len(steps))
        if n >= 2:
            give(n - 2).wait()
        total = jnp.dot(
            rows_ref[m * tile : (m + 1) * tile, :],
            cols[k][...],
            preferred_element_type=jnp.float32,
        )
        tiles[n % 2] = total * scale
        give(n).start()
    for n in range(max(count - 2, 0), count):
        give(n).wait()
    done_ref[...] = jnp.zeros_like(done_ref)


def gram_part(gram, steps, start, cols, rows, shape, scale, after=()):
    genes, depth = rows.shape
    width = cols[0].shape[1]
    tile = min(TILE, genes)
    inner = shape[1] // genes
    operands = [rows, *cols, *after]
    in_specs = [VMEM] * (1 + len(cols)) + [ANY] * len(after)
    aliases = {}
    if gram is not None:
        aliases = {len(operands): 0}
        in_specs.append(ANY)
        operands.append(gram)
    return call(
        functools.partial(gram_kernel, inner, steps, start, scale),
        "gram_part",
        (
            2 * len(cols) * genes * depth * width,
            4 * len(cols) * genes * width + 2 * genes * depth,
            0,
        ),
        vmem=24,
        in_specs=in_specs,
        out_specs=[ANY, VMEM],
        out_shape=[
            jax.ShapeDtypeStruct(shape, jnp.float32),
            jax.ShapeDtypeStruct((8, 128), jnp.float32),
        ],
        scratch_shapes=[
            pltpu.VMEM((2, tile, width), jnp.float32),
            pltpu.SemaphoreType.DMA((2,)),
        ],
        input_output_aliases=aliases,
    )(*operands)


def chunks(genes):
    units, spans, at = genes // STRIP, [], 0
    for share in SHARES[:-1]:
        size = max(1, units * share // sum(SHARES))
        spans.append((at * STRIP, size * STRIP))
        at += size
    return spans + [(at * STRIP, (units - at) * STRIP)]


def shards(counts, gene_mean, gene_std):
    groups = lax.axis_size("cell")
    outer, inner = groups, lax.axis_size("gene") // groups
    cells, genes = counts.shape
    part, counts = count_part(counts)
    terms = library_terms(part, outer * inner)
    scales = gene_scales(gene_mean[None, :], gene_std[None, :], [terms[0]])
    given = counts, scales, terms

    spans, blocks, nears, mine = chunks(genes), [], [], []
    for start, width in spans:
        (block,) = standardize(
            lambda terms, *refs, start=start: block_kernel(terms, start, *refs),
            "standardize_block",
            (cells, width),
            1,
            *given,
            [*mine, *blocks[1:]],
        )
        blocks.append(block)
        nears.append(line_near(block, outer, inner))
        if not mine:
            mine = standardize(
                rows_kernel, "standardize_rows", (genes, cells), 1, *given, [block]
            )
    lines, boths = [], []
    for q, (block, near) in enumerate(zip(blocks, nears)):
        after = boths[-1:] + (nears[q + 1 : q + 2] if q else [])
        both, arrays = line_gather(block, near, outer, inner, after)
        lines.append(arrays)
        boths.append(both)
    rows = stack(row_blocks(mine[0], groups, boths[1:2]))

    shape = (genes, genes * inner)
    scale = 1.0 / (cells * groups)
    across = [[(c, c ^ j) for c in range(groups)] for j in range(groups)]
    swap = [
        [
            (o * inner + (i + s) % inner, o * inner + i)
            for o in range(outer)
            for i in range(inner)
        ]
        for s in range(inner)
    ]
    write = functools.partial(gram_part, rows=rows, shape=shape, scale=scale)
    gram, done, sent, arrived = None, rows, [], []

    def fetch(q):
        ahead = lines[q + 1][2:3] if q + 1 < len(spans) else []
        sends = pick(lines[q], outer, inner, [done] + sent[-1:] + boths[-1:] + ahead)
        sent.append(sends[0])
        cols = [send(sends[j], "cell", across[j]) for j in range(1, groups)]
        arrived.append([sends[0]] + cols)

    fetch(0)
    for q, (start, _) in enumerate(spans):
        if q + 1 < len(spans):
            fetch(q + 1)
        own = stack([arrived[q]], [done] * (q > 0) + sent[q + 1 : q + 2])
        theirs = [send(own, "gene", swap[s]) for s in range(1, inner)]
        parts = list(enumerate([own] + theirs))
        for part in [parts] if q + 1 < len(spans) else [[x] for x in parts]:
            steps, cols = zip(*part)
            gram, done = write(gram, steps, start, cols, after=sent[q + 1 : q + 2])
    return gram


def solution(mesh):
    placed = (P("cell", "gene"), P("gene"), P("gene"))
    return jax.shard_map(
        shards, mesh=mesh, in_specs=placed, out_specs=P("gene", "cell"), check_vma=False
    )
```

```python
import functools

import jax
import jax.numpy as jnp
from jax import lax
from jax.experimental import pallas as pl
from jax.experimental.pallas import tpu as pltpu
from jax.sharding import PartitionSpec as P

STRIP = 128
SHARES = (3, 3, 2)
TILE = 1024
MIB = 2**20
SLACK = 8
VMEM = pl.BlockSpec(memory_space=pltpu.VMEM)
ANY = pl.BlockSpec(memory_space=pl.ANY)


def send(x, axis, pairs):
    return lax.ppermute(x, axis, pairs)


def call(kernel, name, cost, vmem=8, **kwargs):
    flops, moved, transcendentals = cost
    return pl.pallas_call(
        kernel,
        name=name,
        cost_estimate=pl.CostEstimate(
            flops=flops // SLACK,
            bytes_accessed=moved // SLACK,
            transcendentals=transcendentals // SLACK,
        ),
        compiler_params=pltpu.CompilerParams(vmem_limit_bytes=vmem * MIB),
        **kwargs,
    )


def count_kernel(counts_ref, out_ref, held_ref):
    cells, genes = counts_ref.shape
    total = jnp.zeros((cells, STRIP), jnp.float32)
    for at in range(0, genes, STRIP):
        strip = counts_ref[:, at : at + STRIP]
        held_ref[:, at : at + STRIP] = strip
        total += strip
    summed = jnp.sum(total, axis=1, keepdims=True)
    flat = jnp.broadcast_to(summed, (cells, STRIP)).T
    out_ref[...] = flat[:8, :]


def count_part(counts):
    cells, genes = counts.shape
    return call(
        count_kernel,
        "count_part",
        (cells * genes, 8 * cells * genes, 0),
        vmem=4,
        in_specs=[VMEM],
        out_specs=[VMEM] * 2,
        out_shape=[
            jax.ShapeDtypeStruct((8, cells), jnp.float32),
            jax.ShapeDtypeStruct(counts.shape, jnp.float32),
        ],
    )(counts)


def scales_kernel(mean_ref, std_ref, *refs):
    out_ref = refs[-1]
    out_ref[0:1, :] = mean_ref[...]
    out_ref[8:9, :] = 1.0 / jnp.maximum(std_ref[...], 0.1)


def gene_scales(mean, std, after):
    genes = mean.shape[1]
    return call(
        scales_kernel,
        "gene_scales",
        (2 * genes, 72 * genes, 0),
        vmem=1,
        in_specs=[VMEM] * 2 + [ANY] * len(after),
        out_specs=VMEM,
        out_shape=jax.ShapeDtypeStruct((16, genes), jnp.float32),
    )(mean, std, *after)


def add_kernel(a_ref, b_ref, out_ref):
    out_ref[...] = a_ref[...] + b_ref[...]


def add(a, b):
    return call(
        add_kernel,
        "add_terms",
        (a.size, 12 * a.size, 0),
        vmem=1,
        in_specs=[VMEM] * 2,
        out_specs=VMEM,
        out_shape=jax.ShapeDtypeStruct(a.shape, a.dtype),
    )(a, b)


def library_terms(part, size):
    terms, step = [part], 1
    while step < size:
        part = terms[0] if len(terms) == 1 else add(*terms)
        terms = [part, send(part, "gene", [(g, g ^ step) for g in range(size)])]
        step *= 2
    return terms


def scaled_strip(counts_ref, genes_ref, factor, at):
    normal = jnp.log1p(counts_ref[:, at] * factor)
    return jnp.minimum((normal - genes_ref[0:1, at]) * genes_ref[8:9, at], 10.0)


def cell_factor(sums, cells):
    library = sums[0][:1, :]
    for ref in sums[1:]:
        library = library + ref[:1, :]
    return jnp.broadcast_to(10000.0 / library, (STRIP, cells)).T


def block_kernel(terms, start, counts_ref, genes_ref, *refs):
    factor = cell_factor(refs[:terms], counts_ref.shape[0])
    out_ref = refs[-1]

    @pl.loop(0, out_ref.shape[1] // STRIP)
    def _(k):
        there = pl.multiple_of(k * STRIP, STRIP)
        at = pl.ds(start + there, STRIP)
        scaled = scaled_strip(counts_ref, genes_ref, factor, at)
        out_ref[:, pl.ds(there, STRIP)] = scaled.astype(jnp.bfloat16)


def rows_kernel(scale, terms, counts_ref, genes_ref, *refs):
    factor = cell_factor(refs[:terms], counts_ref.shape[0])
    out_ref = refs[-1]

    @pl.loop(0, counts_ref.shape[1] // STRIP)
    def _(k):
        at = pl.ds(pl.multiple_of(k * STRIP, STRIP), STRIP)
        scaled = scaled_strip(counts_ref, genes_ref, factor, at)
        out_ref[at, :] = (scaled.T * scale).astype(jnp.bfloat16)


def standardize(kernel, name, shape, pieces, counts, scales, terms, after=()):
    size = pieces * shape[0] * shape[1]
    return call(
        functools.partial(kernel, len(terms)),
        name,
        (20 * size, 6 * size, size),
        in_specs=[VMEM] * (2 + len(terms)) + [ANY] * len(after),
        out_specs=[VMEM] * pieces,
        out_shape=[jax.ShapeDtypeStruct(shape, jnp.bfloat16)] * pieces,
    )(counts, scales, *terms, *after)


def split_kernel(one_ref, two_ref, *refs):
    top_ref, low_ref = refs[-2:]
    half = top_ref.shape[0]
    top_ref[...] = one_ref[:half, :]
    low_ref[...] = two_ref[half:, :]


def row_blocks(mine, groups, after):
    def cross(x, j):
        return send(x, "cell", [(c, c ^ j) for c in range(groups)])

    if groups != 4:
        return [[mine]] + [[cross(mine, j)] for j in range(1, groups)]
    one, two = cross(mine, 1), cross(mine, 2)
    half = jax.ShapeDtypeStruct((mine.shape[0] // 2, mine.shape[1]), mine.dtype)
    top, low = call(
        split_kernel,
        "split_rows",
        (0, 4 * mine.size, 0),
        vmem=4,
        in_specs=[VMEM] * 2 + [ANY] * len(after),
        out_specs=[VMEM] * 2,
        out_shape=[half] * 2,
    )(one, two, *after)
    return [[mine], [one], [two], [cross(top, 2), cross(low, 1)]]


def stack_kernel(places, *refs):
    out_ref = refs[-1]
    for ref, (line, at) in zip(refs, places):
        high, wide = ref.shape
        out_ref[line : line + high, at : at + wide] = ref[...]


def stack(columns, after=()):
    places, blocks, at = [], [], 0
    for column in columns:
        line = 0
        for x in column:
            places.append((line, at))
            blocks.append(x)
            line += x.shape[0]
        at += column[0].shape[1]
    return call(
        functools.partial(stack_kernel, places),
        "stack_blocks",
        (0, 4 * line * at, 0),
        vmem=4,
        in_specs=[VMEM] * len(blocks) + [ANY] * len(after),
        out_specs=VMEM,
        out_shape=jax.ShapeDtypeStruct((line, at), blocks[0].dtype),
    )(*blocks, *after)


def line_pairs(outer, inner, moves):
    return [(a * inner + i, b * inner + i) for a, b in moves for i in range(inner)]


def line_move(x, outer, inner, moves):
    return send(x, "gene", line_pairs(outer, inner, moves))


def line_near(block, outer, inner):
    if outer == 4:
        return line_move(block, outer, inner, [(0, 1), (1, 0), (2, 3), (3, 2)])
    return line_move(block, outer, inner, [(o, o + 1) for o in range(outer - 1)])


def line_gather(block, near, outer, inner, after):
    def move(x, moves):
        return line_move(x, outer, inner, moves)

    if outer == 4:
        both = stack([[block, near]], after)
        across = move(both, [(1, 2), (2, 1)])
        ends = move(across, [(1, 0), (2, 3)])
        return both, [block, near, across, ends]
    ups, downs = [block, near], [block]
    for h in range(1, outer):
        if h > 1:
            ups.append(move(ups[-1], [(o, o + 1) for o in range(h - 1, outer - 1)]))
        downs.append(move(downs[-1], [(o, o - 1) for o in range(1, outer - h + 1)]))
    return block, [block] + ups[1:] + downs[1:]


def line_place(outer, at, wanted):
    if outer == 4:
        far = {0: (2, 3), 1: (2, 3), 2: (1, 0), 3: (1, 0)}[at]
        if wanted in far:
            return far.index(wanted) + (2 if at in (1, 2) else 4)
        return int(wanted != at)
    if wanted <= at:
        return at - wanted
    return outer - 1 + wanted - at


def pick_kernel(groups, outer, inner, arrays, *refs):
    outs = refs[-groups:]
    depth = outs[0].shape[0]
    sources = [
        (ref, part * depth)
        for ref in refs[:arrays]
        for part in range(ref.shape[0] // depth)
    ]
    cell_at = lax.axis_index("cell")
    line_at = lax.div(lax.axis_index("gene"), jnp.int32(inner))
    pairs = [(o, to) for o in range(outer) for to in range(outer)]
    for j in range(groups):
        here = line_at * outer + lax.bitwise_xor(cell_at, jnp.int32(j))
        for k, (ref, line) in enumerate(sources):
            found = [o * outer + to for o, to in pairs if line_place(outer, o, to) == k]
            match = functools.reduce(jnp.logical_or, [here == x for x in found])

            @pl.when(match)
            def _():
                outs[j][...] = ref[line : line + depth, :]


def pick(arrays, outer, inner, after):
    depth, width = arrays[0].shape
    return call(
        functools.partial(pick_kernel, outer, outer, inner, len(arrays)),
        "pick_blocks",
        (0, 4 * outer * depth * width, 0),
        vmem=4,
        in_specs=[VMEM] * len(arrays) + [ANY] * len(after),
        out_specs=[VMEM] * outer,
        out_shape=[jax.ShapeDtypeStruct((depth, width), arrays[0].dtype)] * outer,
    )(*arrays, *after)


def gram_kernel(inner, steps, start, scale, rows_ref, *refs):
    cols = refs[: len(steps)]
    out_ref, done_ref, tiles, sems = refs[-4:]
    tile, width = tiles.shape[1:]
    genes = rows_ref.shape[0]

    def give(n):
        m, k = divmod(n, len(steps))
        owner = lax.rem(lax.axis_index("gene") + steps[k], jnp.int32(inner))
        at = pl.multiple_of(owner * genes + start, STRIP)
        return pltpu.make_async_copy(
            tiles.at[n % 2],
            out_ref.at[pl.ds(m * tile, tile), pl.ds(at, width)],
            sems.at[n % 2],
        )

    count = genes // tile * len(steps)
    for n in range(count):
        m, k = divmod(n, len(steps))
        if n >= 2:
            give(n - 2).wait()
        total = jnp.dot(
            rows_ref[m * tile : (m + 1) * tile, :],
            cols[k][...],
            preferred_element_type=jnp.float32,
        )
        tiles[n % 2] = total if scale == 1.0 else total * scale
        give(n).start()
    for n in range(max(count - 2, 0), count):
        give(n).wait()
    done_ref[...] = jnp.zeros_like(done_ref)


def gram_part(gram, steps, start, cols, rows, shape, scale, after=()):
    genes, depth = rows.shape
    width = cols[0].shape[1]
    tile = min(TILE, genes)
    inner = shape[1] // genes
    operands = [rows, *cols, *after]
    in_specs = [VMEM] * (1 + len(cols)) + [ANY] * len(after)
    aliases = {}
    if gram is not None:
        aliases = {len(operands): 0}
        in_specs.append(ANY)
        operands.append(gram)
    return call(
        functools.partial(gram_kernel, inner, steps, start, scale),
        "gram_part",
        (
            2 * len(cols) * genes * depth * width,
            4 * len(cols) * genes * width + 2 * genes * depth,
            0,
        ),
        vmem=24,
        in_specs=in_specs,
        out_specs=[ANY, VMEM],
        out_shape=[
            jax.ShapeDtypeStruct(shape, jnp.float32),
            jax.ShapeDtypeStruct((8, 128), jnp.float32),
        ],
        scratch_shapes=[
            pltpu.VMEM((2, tile, width), jnp.float32),
            pltpu.SemaphoreType.DMA((2,)),
        ],
        input_output_aliases=aliases,
    )(*operands)


def chunks(genes):
    units, spans, at = genes // STRIP, [], 0
    for share in SHARES[:-1]:
        size = max(1, units * share // sum(SHARES))
        spans.append((at * STRIP, size * STRIP))
        at += size
    return spans + [(at * STRIP, (units - at) * STRIP)]


def shards(counts, gene_mean, gene_std):
    groups = lax.axis_size("cell")
    outer, inner = groups, lax.axis_size("gene") // groups
    cells, genes = counts.shape
    part, counts = count_part(counts)
    terms = library_terms(part, outer * inner)
    scales = gene_scales(gene_mean[None, :], gene_std[None, :], [terms[0]])
    given = counts, scales, terms

    scale = 1.0 / (cells * groups)
    exact = cells * groups & (cells * groups - 1) == 0
    row_scale, scale = (scale, 1.0) if exact else (1.0, scale)
    spans, blocks, nears, mine = chunks(genes), [], [], []
    for start, width in spans:
        (block,) = standardize(
            lambda terms, *refs, start=start: block_kernel(terms, start, *refs),
            "standardize_block",
            (cells, width),
            1,
            *given,
            [*mine, *blocks[1:]],
        )
        blocks.append(block)
        nears.append(line_near(block, outer, inner))
        if not mine:
            mine = standardize(
                functools.partial(rows_kernel, row_scale),
                "standardize_rows",
                (genes, cells),
                1,
                *given,
                [block],
            )
    lines, boths = [], []
    for q, (block, near) in enumerate(zip(blocks, nears)):
        after = boths[-1:] + (nears[q + 1 :] if q else [])
        both, arrays = line_gather(block, near, outer, inner, after)
        lines.append(arrays)
        boths.append(both)
    rows = stack(row_blocks(mine[0], groups, boths[1:2]))

    shape = (genes, genes * inner)
    across = [[(c, c ^ j) for c in range(groups)] for j in range(groups)]
    swap = [
        [
            (o * inner + (i + s) % inner, o * inner + i)
            for o in range(outer)
            for i in range(inner)
        ]
        for s in range(inner)
    ]
    write = functools.partial(gram_part, rows=rows, shape=shape, scale=scale)
    gram, done, sent, arrived = None, rows, [], []

    def fetch(q):
        ahead = lines[q + 1][2:3] if q + 1 < len(spans) else []
        sends = pick(lines[q], outer, inner, [done] + sent[-1:] + boths[-1:] + ahead)
        sent.append(sends[0])
        cols = [send(sends[j], "cell", across[j]) for j in range(1, groups)]
        arrived.append([sends[0]] + cols)

    fetch(0)
    for q, (start, _) in enumerate(spans):
        if q + 1 < len(spans):
            fetch(q + 1)
        own = stack([arrived[q]], [done] * (q > 0) + sent[q + 1 : q + 2])
        theirs = [send(own, "gene", swap[s]) for s in range(1, inner)]
        parts = list(enumerate([own] + theirs))
        for part in [parts] if q + 1 < len(spans) else [[x] for x in parts]:
            steps, cols = zip(*part)
            gram, done = write(gram, steps, start, cols, after=sent[q + 1 : q + 2])
    return gram


def solution(mesh):
    placed = (P("cell", "gene"), P("gene"), P("gene"))
    return jax.shard_map(
        shards, mesh=mesh, in_specs=placed, out_specs=P("gene", "cell"), check_vma=False
    )
```

```python
import functools

import jax
import jax.numpy as jnp
from jax import lax
from jax.experimental import pallas as pl
from jax.experimental.pallas import tpu as pltpu
from jax.sharding import PartitionSpec as P

STRIP = 128
SHARES = (5, 5, 6)
TILE = 1024
MIB = 2**20
SLACK = 8
VMEM = pl.BlockSpec(memory_space=pltpu.VMEM)
ANY = pl.BlockSpec(memory_space=pl.ANY)


def send(x, axis, pairs):
    return lax.ppermute(x, axis, pairs)


def call(kernel, name, cost, vmem=8, **kwargs):
    flops, moved, transcendentals = cost
    return pl.pallas_call(
        kernel,
        name=name,
        cost_estimate=pl.CostEstimate(
            flops=flops // SLACK,
            bytes_accessed=moved // SLACK,
            transcendentals=transcendentals // SLACK,
        ),
        compiler_params=pltpu.CompilerParams(vmem_limit_bytes=vmem * MIB),
        **kwargs,
    )


def count_kernel(counts_ref, out_ref, held_ref):
    cells, genes = counts_ref.shape
    total = jnp.zeros((cells, STRIP), jnp.float32)
    for at in range(0, genes, STRIP):
        strip = counts_ref[:, at : at + STRIP]
        held_ref[:, at : at + STRIP] = strip
        total += strip
    summed = jnp.sum(total, axis=1, keepdims=True)
    flat = jnp.broadcast_to(summed, (cells, STRIP)).T
    out_ref[...] = flat[:8, :]


def count_part(counts):
    cells, genes = counts.shape
    return call(
        count_kernel,
        "count_part",
        (cells * genes, 8 * cells * genes, 0),
        vmem=4,
        in_specs=[VMEM],
        out_specs=[VMEM] * 2,
        out_shape=[
            jax.ShapeDtypeStruct((8, cells), jnp.float32),
            jax.ShapeDtypeStruct(counts.shape, jnp.float32),
        ],
    )(counts)


def scales_kernel(mean_ref, std_ref, *refs):
    out_ref = refs[-1]
    out_ref[0:1, :] = mean_ref[...]
    out_ref[8:9, :] = 1.0 / jnp.maximum(std_ref[...], 0.1)


def gene_scales(mean, std, after):
    genes = mean.shape[1]
    return call(
        scales_kernel,
        "gene_scales",
        (2 * genes, 72 * genes, 0),
        vmem=1,
        in_specs=[VMEM] * 2 + [ANY] * len(after),
        out_specs=VMEM,
        out_shape=jax.ShapeDtypeStruct((16, genes), jnp.float32),
    )(mean, std, *after)


def add_kernel(a_ref, b_ref, out_ref):
    out_ref[...] = a_ref[...] + b_ref[...]


def add(a, b):
    return call(
        add_kernel,
        "add_terms",
        (a.size, 12 * a.size, 0),
        vmem=1,
        in_specs=[VMEM] * 2,
        out_specs=VMEM,
        out_shape=jax.ShapeDtypeStruct(a.shape, a.dtype),
    )(a, b)


def library_terms(part, size):
    terms, step = [part], 1
    while step < size:
        part = terms[0] if len(terms) == 1 else add(*terms)
        terms = [part, send(part, "gene", [(g, g ^ step) for g in range(size)])]
        step *= 2
    return terms


def scaled_strip(counts_ref, genes_ref, factor, at):
    normal = jnp.log1p(counts_ref[:, at] * factor)
    return jnp.minimum((normal - genes_ref[0:1, at]) * genes_ref[8:9, at], 10.0)


def cell_factor(sums, cells):
    library = sums[0][:1, :]
    for ref in sums[1:]:
        library = library + ref[:1, :]
    return jnp.broadcast_to(10000.0 / library, (STRIP, cells)).T


def block_kernel(terms, start, counts_ref, genes_ref, *refs):
    factor = cell_factor(refs[:terms], counts_ref.shape[0])
    out_ref = refs[-1]

    @pl.loop(0, out_ref.shape[1] // STRIP)
    def _(k):
        there = pl.multiple_of(k * STRIP, STRIP)
        at = pl.ds(start + there, STRIP)
        scaled = scaled_strip(counts_ref, genes_ref, factor, at)
        out_ref[:, pl.ds(there, STRIP)] = scaled.astype(jnp.bfloat16)


def rows_kernel(scale, terms, counts_ref, genes_ref, *refs):
    factor = cell_factor(refs[:terms], counts_ref.shape[0])
    out_ref = refs[-1]

    @pl.loop(0, counts_ref.shape[1] // STRIP)
    def _(k):
        at = pl.ds(pl.multiple_of(k * STRIP, STRIP), STRIP)
        scaled = scaled_strip(counts_ref, genes_ref, factor, at)
        out_ref[at, :] = (scaled.T * scale).astype(jnp.bfloat16)


def standardize(kernel, name, shape, pieces, counts, scales, terms, after=()):
    size = pieces * shape[0] * shape[1]
    return call(
        functools.partial(kernel, len(terms)),
        name,
        (20 * size, 6 * size, size),
        in_specs=[VMEM] * (2 + len(terms)) + [ANY] * len(after),
        out_specs=[VMEM] * pieces,
        out_shape=[jax.ShapeDtypeStruct(shape, jnp.bfloat16)] * pieces,
    )(counts, scales, *terms, *after)


def split_kernel(one_ref, two_ref, *refs):
    top_ref, low_ref = refs[-2:]
    half = top_ref.shape[0]
    top_ref[...] = one_ref[:half, :]
    low_ref[...] = two_ref[half:, :]


def row_blocks(mine, groups, after):
    def cross(x, j):
        return send(x, "cell", [(c, c ^ j) for c in range(groups)])

    if groups != 4:
        return [[mine]] + [[cross(mine, j)] for j in range(1, groups)]
    one, two = cross(mine, 1), cross(mine, 2)
    half = jax.ShapeDtypeStruct((mine.shape[0] // 2, mine.shape[1]), mine.dtype)
    top, low = call(
        split_kernel,
        "split_rows",
        (0, 4 * mine.size, 0),
        vmem=4,
        in_specs=[VMEM] * 2 + [ANY] * len(after),
        out_specs=[VMEM] * 2,
        out_shape=[half] * 2,
    )(one, two, *after)
    return [[mine], [one], [two], [cross(top, 2), cross(low, 1)]]


def stack_kernel(places, *refs):
    out_ref = refs[-1]
    for ref, (line, at) in zip(refs, places):
        high, wide = ref.shape
        out_ref[line : line + high, at : at + wide] = ref[...]


def stack(columns, after=()):
    places, blocks, at = [], [], 0
    for column in columns:
        line = 0
        for x in column:
            places.append((line, at))
            blocks.append(x)
            line += x.shape[0]
        at += column[0].shape[1]
    return call(
        functools.partial(stack_kernel, places),
        "stack_blocks",
        (0, 4 * line * at, 0),
        vmem=4,
        in_specs=[VMEM] * len(blocks) + [ANY] * len(after),
        out_specs=VMEM,
        out_shape=jax.ShapeDtypeStruct((line, at), blocks[0].dtype),
    )(*blocks, *after)


def line_pairs(outer, inner, moves):
    return [(a * inner + i, b * inner + i) for a, b in moves for i in range(inner)]


def line_move(x, outer, inner, moves):
    return send(x, "gene", line_pairs(outer, inner, moves))


def line_near(block, outer, inner):
    if outer == 4:
        return line_move(block, outer, inner, [(0, 1), (1, 0), (2, 3), (3, 2)])
    return line_move(block, outer, inner, [(o, o + 1) for o in range(outer - 1)])


def line_gather(block, near, outer, inner, after):
    def move(x, moves):
        return line_move(x, outer, inner, moves)

    if outer == 4:
        both = stack([[block, near]], after)
        across = move(both, [(1, 2), (2, 1)])
        ends = move(across, [(1, 0), (2, 3)])
        return both, [block, near, across, ends]
    ups, downs = [block, near], [block]
    for h in range(1, outer):
        if h > 1:
            ups.append(move(ups[-1], [(o, o + 1) for o in range(h - 1, outer - 1)]))
        downs.append(move(downs[-1], [(o, o - 1) for o in range(1, outer - h + 1)]))
    return block, [block] + ups[1:] + downs[1:]


def line_place(outer, at, wanted):
    if outer == 4:
        far = {0: (2, 3), 1: (2, 3), 2: (1, 0), 3: (1, 0)}[at]
        if wanted in far:
            return far.index(wanted) + (2 if at in (1, 2) else 4)
        return int(wanted != at)
    if wanted <= at:
        return at - wanted
    return outer - 1 + wanted - at


def pick_kernel(groups, outer, inner, arrays, *refs):
    outs = refs[-groups:]
    depth = outs[0].shape[0]
    sources = [
        (ref, part * depth)
        for ref in refs[:arrays]
        for part in range(ref.shape[0] // depth)
    ]
    cell_at = lax.axis_index("cell")
    line_at = lax.div(lax.axis_index("gene"), jnp.int32(inner))
    pairs = [(o, to) for o in range(outer) for to in range(outer)]
    for j in range(groups):
        here = line_at * outer + lax.bitwise_xor(cell_at, jnp.int32(j))
        for k, (ref, line) in enumerate(sources):
            found = [o * outer + to for o, to in pairs if line_place(outer, o, to) == k]
            match = functools.reduce(jnp.logical_or, [here == x for x in found])

            @pl.when(match)
            def _():
                outs[j][...] = ref[line : line + depth, :]


def pick(arrays, outer, inner, after):
    depth, width = arrays[0].shape
    return call(
        functools.partial(pick_kernel, outer, outer, inner, len(arrays)),
        "pick_blocks",
        (0, 4 * outer * depth * width, 0),
        vmem=4,
        in_specs=[VMEM] * len(arrays) + [ANY] * len(after),
        out_specs=[VMEM] * outer,
        out_shape=[jax.ShapeDtypeStruct((depth, width), arrays[0].dtype)] * outer,
    )(*arrays, *after)


def gram_kernel(inner, steps, start, scale, rows_ref, *refs):
    cols = refs[: len(steps)]
    out_ref, done_ref, tiles, sems = refs[-4:]
    tile, width = tiles.shape[1:]
    genes = rows_ref.shape[0]

    def give(n):
        m, k = divmod(n, len(steps))
        owner = lax.rem(lax.axis_index("gene") + steps[k], jnp.int32(inner))
        at = pl.multiple_of(owner * genes + start, STRIP)
        return pltpu.make_async_copy(
            tiles.at[n % 2],
            out_ref.at[pl.ds(m * tile, tile), pl.ds(at, width)],
            sems.at[n % 2],
        )

    count = genes // tile * len(steps)
    for n in range(count):
        m, k = divmod(n, len(steps))
        if n >= 2:
            give(n - 2).wait()
        total = jnp.dot(
            rows_ref[m * tile : (m + 1) * tile, :],
            cols[k][...],
            preferred_element_type=jnp.float32,
        )
        tiles[n % 2] = total if scale == 1.0 else total * scale
        give(n).start()
    for n in range(max(count - 2, 0), count):
        give(n).wait()
    done_ref[...] = jnp.zeros_like(done_ref)


def gram_part(gram, steps, start, cols, rows, shape, scale, after=()):
    genes, depth = rows.shape
    width = cols[0].shape[1]
    tile = min(TILE, genes)
    inner = shape[1] // genes
    operands = [rows, *cols, *after]
    in_specs = [VMEM] * (1 + len(cols)) + [ANY] * len(after)
    aliases = {}
    if gram is not None:
        aliases = {len(operands): 0}
        in_specs.append(ANY)
        operands.append(gram)
    return call(
        functools.partial(gram_kernel, inner, steps, start, scale),
        "gram_part",
        (
            2 * len(cols) * genes * depth * width,
            4 * len(cols) * genes * width + 2 * genes * depth,
            0,
        ),
        vmem=24,
        in_specs=in_specs,
        out_specs=[ANY, VMEM],
        out_shape=[
            jax.ShapeDtypeStruct(shape, jnp.float32),
            jax.ShapeDtypeStruct((8, 128), jnp.float32),
        ],
        scratch_shapes=[
            pltpu.VMEM((2, tile, width), jnp.float32),
            pltpu.SemaphoreType.DMA((2,)),
        ],
        input_output_aliases=aliases,
    )(*operands)


def chunks(genes):
    units, spans, at = genes // STRIP, [], 0
    for share in SHARES[:-1]:
        size = max(1, units * share // sum(SHARES))
        spans.append((at * STRIP, size * STRIP))
        at += size
    return spans + [(at * STRIP, (units - at) * STRIP)]


def shards(counts, gene_mean, gene_std):
    groups = lax.axis_size("cell")
    outer, inner = groups, lax.axis_size("gene") // groups
    cells, genes = counts.shape
    part, counts = count_part(counts)
    terms = library_terms(part, outer * inner)
    scales = gene_scales(gene_mean[None, :], gene_std[None, :], [terms[0]])
    given = counts, scales, terms

    scale = 1.0 / (cells * groups)
    exact = cells * groups & (cells * groups - 1) == 0
    row_scale, scale = (scale, 1.0) if exact else (1.0, scale)
    spans, blocks, nears, mine = chunks(genes), [], [], []
    for start, width in spans:
        (block,) = standardize(
            lambda terms, *refs, start=start: block_kernel(terms, start, *refs),
            "standardize_block",
            (cells, width),
            1,
            *given,
            [*mine, *blocks[1:]],
        )
        blocks.append(block)
        nears.append(line_near(block, outer, inner))
        if not mine:
            mine = standardize(
                functools.partial(rows_kernel, row_scale),
                "standardize_rows",
                (genes, cells),
                1,
                *given,
                [block],
            )
    lines, boths = [], []
    for q, (block, near) in enumerate(zip(blocks, nears)):
        after = boths[-1:] + (nears[q + 1 :] if q else [])
        both, arrays = line_gather(block, near, outer, inner, after)
        lines.append(arrays)
        boths.append(both)
    rows = stack(row_blocks(mine[0], groups, boths[1:2]))

    shape = (genes, genes * inner)
    across = [[(c, c ^ j) for c in range(groups)] for j in range(groups)]
    swap = [
        [
            (o * inner + (i + s) % inner, o * inner + i)
            for o in range(outer)
            for i in range(inner)
        ]
        for s in range(inner)
    ]
    write = functools.partial(gram_part, rows=rows, shape=shape, scale=scale)
    gram, done, sent, arrived = None, rows, [], []

    def fetch(q):
        ahead = lines[q + 1][2:3] if q + 1 < len(spans) else []
        sends = pick(lines[q], outer, inner, [done] + sent[-1:] + boths[-1:] + ahead)
        sent.append(sends[0])
        cols = [send(sends[j], "cell", across[j]) for j in range(1, groups)]
        arrived.append([sends[0]] + cols)

    fetch(0)
    for q, (start, _) in enumerate(spans):
        if q + 1 < len(spans):
            fetch(q + 1)
        own = stack([arrived[q]], [done] * (q > 0) + sent[q + 1 : q + 2])
        theirs = [send(own, "gene", swap[s]) for s in range(1, inner)]
        parts = list(enumerate([own] + theirs))
        for part in [parts] if q + 1 < len(spans) else [[x] for x in parts]:
            steps, cols = zip(*part)
            gram, done = write(gram, steps, start, cols, after=sent[q + 1 : q + 2])
    return gram


def solution(mesh):
    placed = (P("cell", "gene"), P("gene"), P("gene"))
    return jax.shard_map(
        shards, mesh=mesh, in_specs=placed, out_specs=P("gene", "cell"), check_vma=False
    )
```

```python
import functools

import jax
import jax.numpy as jnp
from jax import lax
from jax.experimental import pallas as pl
from jax.experimental.pallas import tpu as pltpu
from jax.sharding import PartitionSpec as P

STRIP = 128
SHARES = (5, 5, 6)
TILE = 1024
MIB = 2**20
SLACK = 8
VMEM = pl.BlockSpec(memory_space=pltpu.VMEM)
ANY = pl.BlockSpec(memory_space=pl.ANY)


def send(x, axis, pairs):
    return lax.ppermute(x, axis, pairs)


def call(kernel, name, cost, vmem=8, **kwargs):
    flops, moved, transcendentals = cost
    return pl.pallas_call(
        kernel,
        name=name,
        cost_estimate=pl.CostEstimate(
            flops=flops // SLACK,
            bytes_accessed=moved // SLACK,
            transcendentals=transcendentals // SLACK,
        ),
        compiler_params=pltpu.CompilerParams(vmem_limit_bytes=vmem * MIB),
        **kwargs,
    )


def count_kernel(counts_ref, out_ref, held_ref):
    cells, genes = counts_ref.shape
    total = jnp.zeros((cells, STRIP), jnp.float32)
    for at in range(0, genes, STRIP):
        strip = counts_ref[:, at : at + STRIP]
        held_ref[:, at : at + STRIP] = strip
        total += strip
    summed = jnp.sum(total, axis=1, keepdims=True)
    flat = jnp.broadcast_to(summed, (cells, STRIP)).T
    out_ref[...] = flat[:8, :]


def count_part(counts):
    cells, genes = counts.shape
    return call(
        count_kernel,
        "count_part",
        (cells * genes, 8 * cells * genes, 0),
        vmem=4,
        in_specs=[VMEM],
        out_specs=[VMEM] * 2,
        out_shape=[
            jax.ShapeDtypeStruct((8, cells), jnp.float32),
            jax.ShapeDtypeStruct(counts.shape, jnp.float32),
        ],
    )(counts)


def scales_kernel(mean_ref, std_ref, *refs):
    out_ref = refs[-1]
    out_ref[0:1, :] = mean_ref[...]
    out_ref[8:9, :] = 1.0 / jnp.maximum(std_ref[...], 0.1)


def gene_scales(mean, std, after):
    genes = mean.shape[1]
    return call(
        scales_kernel,
        "gene_scales",
        (2 * genes, 72 * genes, 0),
        vmem=1,
        in_specs=[VMEM] * 2 + [ANY] * len(after),
        out_specs=VMEM,
        out_shape=jax.ShapeDtypeStruct((16, genes), jnp.float32),
    )(mean, std, *after)


def add_kernel(a_ref, b_ref, out_ref):
    out_ref[...] = a_ref[...] + b_ref[...]


def add(a, b):
    return call(
        add_kernel,
        "add_terms",
        (a.size, 12 * a.size, 0),
        vmem=1,
        in_specs=[VMEM] * 2,
        out_specs=VMEM,
        out_shape=jax.ShapeDtypeStruct(a.shape, a.dtype),
    )(a, b)


def library_terms(part, size):
    terms, step = [part], 1
    while step < size:
        part = terms[0] if len(terms) == 1 else add(*terms)
        terms = [part, send(part, "gene", [(g, g ^ step) for g in range(size)])]
        step *= 2
    return terms


def scaled_strip(counts_ref, genes_ref, factor, at):
    normal = jnp.log1p(counts_ref[:, at] * factor)
    return jnp.minimum((normal - genes_ref[0:1, at]) * genes_ref[8:9, at], 10.0)


def cell_factor(sums, cells):
    library = sums[0][:1, :]
    for ref in sums[1:]:
        library = library + ref[:1, :]
    return jnp.broadcast_to(10000.0 / library, (STRIP, cells)).T


def block_kernel(terms, start, counts_ref, genes_ref, *refs):
    factor = cell_factor(refs[:terms], counts_ref.shape[0])
    out_ref = refs[-1]

    @pl.loop(0, out_ref.shape[1] // STRIP)
    def _(k):
        there = pl.multiple_of(k * STRIP, STRIP)
        at = pl.ds(start + there, STRIP)
        scaled = scaled_strip(counts_ref, genes_ref, factor, at)
        out_ref[:, pl.ds(there, STRIP)] = scaled.astype(jnp.bfloat16)


def rows_kernel(scale, terms, counts_ref, genes_ref, *refs):
    factor = cell_factor(refs[:terms], counts_ref.shape[0])
    out_ref = refs[-1]

    @pl.loop(0, counts_ref.shape[1] // STRIP)
    def _(k):
        at = pl.ds(pl.multiple_of(k * STRIP, STRIP), STRIP)
        scaled = scaled_strip(counts_ref, genes_ref, factor, at)
        out_ref[at, :] = (scaled.T * scale).astype(jnp.bfloat16)


def standardize(kernel, name, shape, pieces, counts, scales, terms, after=()):
    size = pieces * shape[0] * shape[1]
    return call(
        functools.partial(kernel, len(terms)),
        name,
        (20 * size, 6 * size, size),
        in_specs=[VMEM] * (2 + len(terms)) + [ANY] * len(after),
        out_specs=[VMEM] * pieces,
        out_shape=[jax.ShapeDtypeStruct(shape, jnp.bfloat16)] * pieces,
    )(counts, scales, *terms, *after)


def split_kernel(one_ref, two_ref, *refs):
    top_ref, low_ref = refs[-2:]
    half = top_ref.shape[0]
    top_ref[...] = one_ref[:half, :]
    low_ref[...] = two_ref[half:, :]


def row_blocks(mine, groups, after):
    def cross(x, j):
        return send(x, "cell", [(c, c ^ j) for c in range(groups)])

    if groups != 4:
        return [[mine]] + [[cross(mine, j)] for j in range(1, groups)]
    one, two = cross(mine, 1), cross(mine, 2)
    half = jax.ShapeDtypeStruct((mine.shape[0] // 2, mine.shape[1]), mine.dtype)
    top, low = call(
        split_kernel,
        "split_rows",
        (0, 4 * mine.size, 0),
        vmem=4,
        in_specs=[VMEM] * 2 + [ANY] * len(after),
        out_specs=[VMEM] * 2,
        out_shape=[half] * 2,
    )(one, two, *after)
    return [[mine], [one], [two], [cross(top, 2), cross(low, 1)]]


def stack_kernel(places, *refs):
    out_ref = refs[-1]
    for ref, (line, at) in zip(refs, places):
        high, wide = ref.shape
        out_ref[line : line + high, at : at + wide] = ref[...]


def stack(columns, after=()):
    places, blocks, at = [], [], 0
    for column in columns:
        line = 0
        for x in column:
            places.append((line, at))
            blocks.append(x)
            line += x.shape[0]
        at += column[0].shape[1]
    return call(
        functools.partial(stack_kernel, places),
        "stack_blocks",
        (0, 4 * line * at, 0),
        vmem=4,
        in_specs=[VMEM] * len(blocks) + [ANY] * len(after),
        out_specs=VMEM,
        out_shape=jax.ShapeDtypeStruct((line, at), blocks[0].dtype),
    )(*blocks, *after)


def line_pairs(outer, inner, moves):
    return [(a * inner + i, b * inner + i) for a, b in moves for i in range(inner)]


def line_move(x, outer, inner, moves):
    return send(x, "gene", line_pairs(outer, inner, moves))


def line_near(block, outer, inner):
    if outer == 4:
        return line_move(block, outer, inner, [(0, 1), (1, 0), (2, 3), (3, 2)])
    return line_move(block, outer, inner, [(o, o + 1) for o in range(outer - 1)])


def line_gather(block, near, outer, inner, after):
    def move(x, moves):
        return line_move(x, outer, inner, moves)

    if outer == 4:
        both = stack([[block, near]], after)
        across = move(both, [(1, 2), (2, 1)])
        ends = move(across, [(1, 0), (2, 3)])
        return both, [block, near, across, ends]
    ups, downs = [block, near], [block]
    for h in range(1, outer):
        if h > 1:
            ups.append(move(ups[-1], [(o, o + 1) for o in range(h - 1, outer - 1)]))
        downs.append(move(downs[-1], [(o, o - 1) for o in range(1, outer - h + 1)]))
    return block, [block] + ups[1:] + downs[1:]


def line_place(outer, at, wanted):
    if outer == 4:
        far = {0: (2, 3), 1: (2, 3), 2: (1, 0), 3: (1, 0)}[at]
        if wanted in far:
            return far.index(wanted) + (2 if at in (1, 2) else 4)
        return int(wanted != at)
    if wanted <= at:
        return at - wanted
    return outer - 1 + wanted - at


def pick_kernel(groups, outer, inner, arrays, first, *refs):
    outs = refs[-groups:]
    depth, width = outs[0].shape
    sources = [
        (ref, part * depth)
        for ref in refs[:arrays]
        for part in range(ref.shape[0] // depth)
    ]
    cell_at = lax.axis_index("cell")
    line_at = lax.div(lax.axis_index("gene"), jnp.int32(inner))
    pairs = [(o, to) for o in range(outer) for to in range(outer)]
    for j in range(groups):
        here = line_at * outer + lax.bitwise_xor(cell_at, jnp.int32(j))
        for k, (ref, line) in enumerate(sources):
            found = [o * outer + to for o, to in pairs if line_place(outer, o, to) == k]
            match = functools.reduce(jnp.logical_or, [here == x for x in found])

            @pl.when(match)
            def _():
                outs[j][...] = ref[line : line + depth, first : first + width]


def pick(arrays, outer, inner, first, width, after):
    depth = arrays[0].shape[0]
    return call(
        functools.partial(pick_kernel, outer, outer, inner, len(arrays), first),
        "pick_blocks",
        (0, 4 * outer * depth * width, 0),
        vmem=4,
        in_specs=[VMEM] * len(arrays) + [ANY] * len(after),
        out_specs=[VMEM] * outer,
        out_shape=[jax.ShapeDtypeStruct((depth, width), arrays[0].dtype)] * outer,
    )(*arrays, *after)


def gram_kernel(inner, steps, start, scale, rows_ref, *refs):
    cols = refs[: len(steps)]
    out_ref, done_ref, tiles, sems = refs[-4:]
    tile, width = tiles.shape[1:]
    genes = rows_ref.shape[0]

    def give(n):
        m, k = divmod(n, len(steps))
        owner = lax.rem(lax.axis_index("gene") + steps[k], jnp.int32(inner))
        at = pl.multiple_of(owner * genes + start, STRIP)
        return pltpu.make_async_copy(
            tiles.at[n % 2],
            out_ref.at[pl.ds(m * tile, tile), pl.ds(at, width)],
            sems.at[n % 2],
        )

    count = genes // tile * len(steps)
    for n in range(count):
        m, k = divmod(n, len(steps))
        if n >= 2:
            give(n - 2).wait()
        total = jnp.dot(
            rows_ref[m * tile : (m + 1) * tile, :],
            cols[k][...],
            preferred_element_type=jnp.float32,
        )
        tiles[n % 2] = total if scale == 1.0 else total * scale
        give(n).start()
    for n in range(max(count - 2, 0), count):
        give(n).wait()
    done_ref[...] = jnp.zeros_like(done_ref)


def gram_part(gram, steps, start, cols, rows, shape, scale, after=()):
    genes, depth = rows.shape
    width = cols[0].shape[1]
    tile = min(TILE, genes)
    inner = shape[1] // genes
    operands = [rows, *cols, *after]
    in_specs = [VMEM] * (1 + len(cols)) + [ANY] * len(after)
    aliases = {}
    if gram is not None:
        aliases = {len(operands): 0}
        in_specs.append(ANY)
        operands.append(gram)
    return call(
        functools.partial(gram_kernel, inner, steps, start, scale),
        "gram_part",
        (
            2 * len(cols) * genes * depth * width,
            4 * len(cols) * genes * width + 2 * genes * depth,
            0,
        ),
        vmem=24,
        in_specs=in_specs,
        out_specs=[ANY, VMEM],
        out_shape=[
            jax.ShapeDtypeStruct(shape, jnp.float32),
            jax.ShapeDtypeStruct((8, 128), jnp.float32),
        ],
        scratch_shapes=[
            pltpu.VMEM((2, tile, width), jnp.float32),
            pltpu.SemaphoreType.DMA((2,)),
        ],
        input_output_aliases=aliases,
    )(*operands)


def chunks(genes):
    units, spans, at = genes // STRIP, [], 0
    for share in SHARES[:-1]:
        size = max(1, units * share // sum(SHARES))
        spans.append((at * STRIP, size * STRIP))
        at += size
    return spans + [(at * STRIP, (units - at) * STRIP)]


def shards(counts, gene_mean, gene_std):
    groups = lax.axis_size("cell")
    outer, inner = groups, lax.axis_size("gene") // groups
    cells, genes = counts.shape
    part, counts = count_part(counts)
    terms = library_terms(part, outer * inner)
    scales = gene_scales(gene_mean[None, :], gene_std[None, :], [terms[0]])
    given = counts, scales, terms

    scale = 1.0 / (cells * groups)
    exact = cells * groups & (cells * groups - 1) == 0
    row_scale, scale = (scale, 1.0) if exact else (1.0, scale)
    spans, blocks, nears, mine = chunks(genes), [], [], []
    for start, width in spans:
        (block,) = standardize(
            lambda terms, *refs, start=start: block_kernel(terms, start, *refs),
            "standardize_block",
            (cells, width),
            1,
            *given,
            [*mine, *blocks[1:]],
        )
        blocks.append(block)
        nears.append(line_near(block, outer, inner))
        if not mine:
            mine = standardize(
                functools.partial(rows_kernel, row_scale),
                "standardize_rows",
                (genes, cells),
                1,
                *given,
                [block],
            )
    lines, boths = [], []
    for q, (block, near) in enumerate(zip(blocks, nears)):
        after = boths[-1:] + (nears[q + 1 :] if q else [])
        both, arrays = line_gather(block, near, outer, inner, after)
        lines.append(arrays)
        boths.append(both)
    rows = stack(row_blocks(mine[0], groups, boths[1:2]))

    shape = (genes, genes * inner)
    across = [[(c, c ^ j) for c in range(groups)] for j in range(groups)]
    swap = [
        [
            (o * inner + (i + s) % inner, o * inner + i)
            for o in range(outer)
            for i in range(inner)
        ]
        for s in range(inner)
    ]
    write = functools.partial(gram_part, rows=rows, shape=shape, scale=scale)
    gram, done, sent, arrived = None, rows, [], []

    pieces = [(q, 0, width) for q, (_, width) in enumerate(spans)]
    q, _, width = pieces.pop()
    cut = width // STRIP * 2 // 3 * STRIP
    pieces += [(q, 0, cut), (q, cut, width - cut)] if cut else [(q, 0, width)]

    def fetch(k):
        q, first, width = pieces[k]
        after = sent[-1:] + boths[-1:]
        if first == 0:
            after += [done] + [arrays[2] for arrays in lines[q + 1 : q + 2]]
        sends = pick(lines[q], outer, inner, first, width, after)
        sent.append(sends[0])
        cols = [send(sends[j], "cell", across[j]) for j in range(1, groups)]
        arrived.append([sends[0]] + cols)

    fetch(0)
    for k, (q, first, _) in enumerate(pieces):
        if k + 1 < len(pieces):
            fetch(k + 1)
        own = stack([arrived[k]], [done] * (k > 0) + sent[k + 1 : k + 2])
        theirs = [send(own, "gene", swap[s]) for s in range(1, inner)]
        parts = list(enumerate([own] + theirs))
        for part in [parts] if k + 1 < len(pieces) else [[x] for x in parts]:
            steps, cols = zip(*part)
            start = spans[q][0] + first
            gram, done = write(gram, steps, start, cols, after=sent[k + 1 : k + 2])
    return gram


def solution(mesh):
    placed = (P("cell", "gene"), P("gene"), P("gene"))
    return jax.shard_map(
        shards, mesh=mesh, in_specs=placed, out_specs=P("gene", "cell"), check_vma=False
    )
```
